512 devices in a mesh: dp: 8 (over x, core), blk: 64 (over y, z).
Axes of the slice: x: 4, y: 8, z: 8, core: 2. Of those that a mesh axis runs over, the one named last changes fastest.
Arguments:
- inputs: bfloat16 [1536, 8192], P('dp', 'blk'), may hold values from -6 to 6
- upstream: bfloat16 [1536, 8192], P('dp', 'blk'), may hold values from -6 to 6
- w_in: bfloat16 [256, 16, 128, 128], P('blk'), may hold values from -0.125 to 0.125
- cols_in: int32 [256, 16], P('blk'), may hold values from 0 to 63, as said below
- w_out: bfloat16 [256, 16, 128, 128], P('blk'), may hold values from -0.0625 to 0.0625
- cols_out: int32 [256, 16], P('blk'), may hold values from 0 to 63, as said below
Outputs:
- grad_inputs: bfloat16 [1536, 8192], P('dp', 'blk')
- grad_w_in: bfloat16 [256, 16, 128, 128], P('blk', 'dp')
- grad_w_out: bfloat16 [256, 16, 128, 128], P('blk', 'dp')
The draws below stay inside these ranges and needn't reach their ends.
Inputs may be any that keep to these rules, and one draw needn't show every extreme that they name: `cols_in`: each block row lists 16 distinct feature blocks. `cols_out`: each block row lists 16 distinct feature blocks.
All inputs are finite; a program needn't handle non-finite values.
Results may differ from the reference program's by a relative error of at most 0.017.
Values may be sent and summed in bfloat16 or wider, within the bound.
No kernel may reach another device: no remote copies, remote signals or barrier semaphores. Data moves between devices by JAX's collectives and lax.ppermute only.
A program may use at most 128 MiB of HBM per device.

```python
import jax
import jax.numpy as jnp
from jax import lax

BLOCK = 128
D = 8192
FF = 32768
TOK = 192
ND = 64
NF = 256
K = 16
TOKENS = 1536
N_DP = 8


def draw_cols_in(key, part):
    key = jax.random.fold_in(key, 11)
    keys = jax.random.split(key, NF)
    return jax.vmap(lambda sub: jax.random.permutation(sub, ND)[:K])(keys).astype(jnp.int32)


def draw_cols_out(key, part):
    key = jax.random.fold_in(key, 23)
    keys = jax.random.split(key, NF)
    return jax.vmap(lambda sub: jax.random.permutation(sub, ND)[:K])(keys).astype(jnp.int32)


def steps_of(rng, extent, cuts, least, high):
    def one(axis_at, shards_of):
        heights = jax.random.uniform(jax.random.fold_in(jax.random.fold_in(rng, 6), axis_at), (shards_of,), jnp.float32, least / len(cuts), high / len(cuts))
        return jnp.repeat(jnp.exp(heights), extent[axis_at] // shards_of).reshape((-1,) + (1,) * (len(extent) - axis_at - 1))

    level = one(*cuts[0])
    for cut in cuts[1:]:
        level = level * one(*cut)
    return level


def bell_draw(rng, shape, spread, bound, cuts=(), kind=jnp.bfloat16):
    gain = steps_of(rng, shape, cuts, -0.22, 0.18) if cuts else 1.0
    array = jax.random.normal(rng, shape, jnp.float32) * spread * gain
    return jnp.minimum(jnp.maximum(array, -bound), bound).astype(kind)


def setup_inputs(seed: int = 0) -> dict:
    key_list = jax.random.split(jax.random.key(seed), 7)
    return {
        "inputs": bell_draw(key_list[0], (TOKENS, D), 1.0, 6.0, ((0, 8), (1, 64))),
        "upstream": bell_draw(key_list[1], (TOKENS, D), 1.0, 6.0, ((0, 8), (1, 64))),
        "w_in": bell_draw(key_list[2], (NF, K, BLOCK, BLOCK), (K * BLOCK) ** -0.5, 0.125, ((0, 64),)),
        "cols_in": draw_cols_in(jax.random.fold_in(key_list[6], 71), 0),
        "w_out": bell_draw(key_list[4], (NF, K, BLOCK, BLOCK), (FF // 4) ** -0.5, 0.0625, ((0, 64),)),
        "cols_out": draw_cols_out(jax.random.fold_in(key_list[6], 71), 0),
    }


def gelu_tanh(values):
    return jax.nn.gelu(values, approximate=True)

def round_trip(values):
    return lax.optimization_barrier(values.astype(jnp.bfloat16)).astype(jnp.float32)

def reference(inputs, upstream, w_in, cols_in, w_out, cols_out):
    in_cols = inputs.reshape(TOKENS, ND, BLOCK)
    up_cols = upstream.reshape(TOKENS, ND, BLOCK)
    stride = 4

    def step(carry, pieces):
        weights_in, index_in, weights_out, index_out = pieces
        in_blocks = in_cols[:, index_in].astype(jnp.float32)
        hidden = jnp.einsum('trki,rkih->trh', in_blocks, weights_in.astype(jnp.float32))
        activated = gelu_tanh(hidden).astype(jnp.bfloat16)
        up_blocks = up_cols[:, index_out].astype(jnp.float32)
        grad_act = jnp.einsum('trko,rkho->trh', up_blocks, weights_out.astype(jnp.float32))
        unused, pull_back = jax.vjp(gelu_tanh, hidden)
        grad_hidden = pull_back(grad_act)[0].astype(jnp.bfloat16)
        act_groups = activated.astype(jnp.float32).reshape(N_DP, TOK, stride, BLOCK)
        grad_groups = grad_hidden.astype(jnp.float32).reshape(N_DP, TOK, stride, BLOCK)
        part_out = jnp.einsum('gtrh,gtrko->grkho', act_groups, up_blocks.reshape(N_DP, TOK, stride, K, BLOCK))
        part_in = jnp.einsum('gtrki,gtrh->grkih', in_blocks.reshape(N_DP, TOK, stride, K, BLOCK), grad_groups)
        rows_out = lax.optimization_barrier(jnp.sum(round_trip(part_out), axis=0)).astype(jnp.bfloat16)
        rows_in = lax.optimization_barrier(jnp.sum(round_trip(part_in), axis=0)).astype(jnp.bfloat16)
        terms = jnp.einsum('trh,rkih->trki', grad_hidden.astype(jnp.float32), weights_in.astype(jnp.float32))
        picks = (index_in[:, :, None] == jnp.arange(ND, dtype=jnp.int32)[None, None, :]).astype(jnp.float32)
        carry = carry + jnp.einsum('trki,rkc->tci', terms, picks, precision=lax.Precision.HIGHEST)
        return (carry, (rows_in, rows_out))
    pieces = (w_in.reshape(NF // stride, stride, K, BLOCK, BLOCK), cols_in.reshape(NF // stride, stride, K), w_out.reshape(NF // stride, stride, K, BLOCK, BLOCK), cols_out.reshape(NF // stride, stride, K))
    start = jnp.zeros((TOKENS, ND, BLOCK), jnp.float32)
    total, grads = lax.scan(step, start, pieces)
    grad_w_in = grads[0].reshape(NF, K, BLOCK, BLOCK)
    grad_w_out = grads[1].reshape(NF, K, BLOCK, BLOCK)
    return (total.reshape(TOKENS, D).astype(jnp.bfloat16), grad_w_in, grad_w_out)
```

```python
import functools

import jax
import jax.numpy as jnp
from jax import lax
from jax.experimental import pallas as pl
from jax.experimental.pallas import tpu as pltpu
from jax.sharding import Mesh, PartitionSpec as P

BF16 = jnp.bfloat16
F32 = jnp.float32
GELU_SCALE = 0.7978845608028654
GELU_CUBE = 0.044715


def dot_nn(a, b):
    return lax.dot_general(a, b, (((1,), (0,)), ((), ())), preferred_element_type=F32)


def dot_nt(a, b):
    return lax.dot_general(a, b, (((1,), (1,)), ((), ())), preferred_element_type=F32)


def dot_tn(a, b):
    return lax.dot_general(a, b, (((0,), (0,)), ((), ())), preferred_element_type=F32)


def act_kernel(cols_in, cols_out, xy, w_in, w_out, placed, act, grad, total):
    rows, per_row, width, _ = w_in.shape
    total[...] = jnp.zeros_like(total)
    for r in range(rows):
        x_row = jnp.concatenate([xy[cols_in[r, k], 0] for k in range(per_row)], axis=1)
        hidden = dot_nn(x_row, w_in[r].reshape(per_row * width, width))
        y_row = jnp.concatenate([xy[cols_out[r, k], 1] for k in range(per_row)], axis=1)
        w_row = jnp.concatenate([w_out[r, k] for k in range(per_row)], axis=1)
        grad_act = dot_nt(y_row, w_row)
        square = hidden * hidden
        tanh = jnp.tanh(GELU_SCALE * hidden * (1.0 + GELU_CUBE * square))
        half = 0.5 * (1.0 + tanh)
        act[r] = (hidden * half).astype(BF16)
        slope = half + 0.5 * hidden * (1.0 - tanh * tanh) * (
            GELU_SCALE * (1.0 + 3.0 * GELU_CUBE * square)
        )
        grad_hidden = (grad_act * slope).astype(BF16)
        grad[r] = grad_hidden
        for k in range(per_row):
            c = cols_in[r, k]
            total[c] = total[c] + dot_nt(grad_hidden, w_in[r, k])
    placed[...] = total[...].astype(BF16)


def weight_kernel(cols_in, cols_out, xy, act, grad, parts):
    cores, xs, _, rows, each, width, _ = parts.shape
    per_row = cores * xs * each
    for r in range(rows):
        act_t = act[r].T
        grad_r = grad[r]
        for k in range(per_row):
            x_at, rest = divmod(k, cores * each)
            c_at, j = divmod(rest, each)
            parts[c_at, x_at, 0, r, j] = dot_tn(xy[cols_in[r, k], 0], grad_r).astype(BF16)
            parts[c_at, x_at, 1, r, j] = dot_nn(act_t, xy[cols_out[r, k], 1]).astype(BF16)


def per_device(sizes, inputs, upstream, w_in, cols_in, w_out, cols_out):
    nx, nc, ny, nz = sizes
    tok, width = inputs.shape
    rows, per_row = cols_in.shape
    each = per_row // (nx * nc)
    blocks = ny * nz
    smem = pl.BlockSpec(memory_space=pltpu.SMEM)
    vmem = pl.BlockSpec(memory_space=pltpu.VMEM)
    params = pltpu.CompilerParams(vmem_limit_bytes=48 * 1024 * 1024)

    xy = lax.all_gather(jnp.stack([inputs, upstream]), ("y", "z"), axis=0, tiled=False)
    placed, act, grad = pl.pallas_call(
        act_kernel,
        out_shape=(
            jax.ShapeDtypeStruct((blocks, tok, width), BF16),
            jax.ShapeDtypeStruct((rows, tok, width), BF16),
            jax.ShapeDtypeStruct((rows, tok, width), BF16),
        ),
        in_specs=[smem, smem, vmem, vmem, vmem],
        out_specs=(vmem, vmem, vmem),
        scratch_shapes=[pltpu.VMEM((blocks, tok, width), F32)],
        compiler_params=params,
        name="act",
    )(cols_in, cols_out, xy, w_in, w_out)

    over_y = lax.psum_scatter(
        placed.reshape(ny, nz * tok, width), "y", scatter_dimension=0, tiled=False
    )

    parts = pl.pallas_call(
        weight_kernel,
        out_shape=jax.ShapeDtypeStruct((nc, nx, 2, rows, each, width, width), BF16),
        in_specs=[smem, smem, vmem, vmem, vmem],
        out_specs=vmem,
        compiler_params=params,
        name="weights",
    )(cols_in, cols_out, xy, act, grad)
    swapped = lax.all_to_all(parts, "c", split_axis=0, concat_axis=0, tiled=True)
    paired = jnp.sum(swapped.astype(F32), axis=0).astype(BF16)
    spread = lax.all_to_all(paired, "x", split_axis=0, concat_axis=0, tiled=True)
    summed = jnp.sum(spread.astype(F32), axis=0).astype(BF16)

    over_y, summed = lax.optimization_barrier((over_y, summed))
    over_y = over_y.reshape(nz, tok, width)
    received = lax.all_to_all(over_y, "z", split_axis=0, concat_axis=0, tiled=True)
    grad_inputs = jnp.sum(received.astype(F32), axis=0).astype(BF16)
    return grad_inputs, summed[0], summed[1]


def solution(mesh):
    n_dp, n_blk = mesh.devices.shape
    sizes = (n_dp // 2, 2, 8, n_blk // 8)
    fine = Mesh(mesh.devices.reshape(sizes), ("x", "c", "y", "z"))
    dp, blk = ("x", "c"), ("y", "z")
    return jax.shard_map(
        functools.partial(per_device, sizes),
        mesh=fine,
        in_specs=(
            P(dp, blk),
            P(dp, blk),
            P(blk, None, None, None),
            P(blk, None),
            P(blk, None, None, None),
            P(blk, None),
        ),
        out_specs=(P(dp, blk), P(blk, dp, None, None), P(blk, dp, None, None)),
        check_vma=False,
    )
```

```python
import functools

import jax
import jax.numpy as jnp
from jax import lax
from jax.experimental import pallas as pl
from jax.experimental.pallas import tpu as pltpu
from jax.sharding import Mesh, PartitionSpec as P

BF16 = jnp.bfloat16
F32 = jnp.float32
GELU_SCALE = 0.7978845608028654
GELU_CUBE = 0.044715
VMEM_LIMIT = 32 * 1024 * 1024
SLABS = 8


def dot_nn(a, b):
    return lax.dot_general(a, b, (((1,), (0,)), ((), ())), preferred_element_type=F32)


def dot_nt(a, b):
    return lax.dot_general(a, b, (((1,), (1,)), ((), ())), preferred_element_type=F32)


def dot_tn(a, b):
    return lax.dot_general(a, b, (((0,), (0,)), ((), ())), preferred_element_type=F32)


def start_loads(xy, x, y, sem):
    slab = xy.shape[0] // SLABS
    both = []
    for which, into in ((0, x), (1, y)):
        ats = [pl.ds(s * slab, slab) for s in range(SLABS)]
        both.append(
            [
                pltpu.make_async_copy(xy.at[at, which], into.at[at], sem.at[which * SLABS + s])
                for s, at in enumerate(ats)
            ]
        )
        for copy in both[-1]:
            copy.start()
    return both


def act_kernel(
    where, xy, w_in, w_out, placed, act, grad, x, y, wi, wo, total, rounded, slope, in_sem, w_sem, out_sem
):
    rows, per_row, width, _ = w_in.shape
    blocks = total.shape[0]
    load_in = pltpu.make_async_copy(w_in, wi, w_sem.at[0])
    load_out = pltpu.make_async_copy(w_out, wo, w_sem.at[1])
    load_in.start()
    load_x, load_y = start_loads(xy, x, y, in_sem)
    load_out.start()
    total[...] = jnp.zeros_like(total)
    load_in.wait()
    for copy in load_x:
        copy.wait()
    for r in range(rows):
        x_row = jnp.concatenate([x[where[0, r * per_row + k]] for k in range(per_row)], axis=1)
        hidden = dot_nn(x_row, wi[r].reshape(per_row * width, width))
        square = hidden * hidden
        tanh = jnp.tanh(GELU_SCALE * hidden * (1.0 + GELU_CUBE * square))
        half = 0.5 * (1.0 + tanh)
        act[r] = (hidden * half).astype(BF16)
        slope[r] = half + 0.5 * hidden * (1.0 - tanh * tanh) * (
            GELU_SCALE * (1.0 + 3.0 * GELU_CUBE * square)
        )
    for copy in load_y:
        copy.wait()
    load_out.wait()
    for r in range(rows):
        y_row = jnp.concatenate([y[where[1, r * per_row + k]] for k in range(per_row)], axis=1)
        w_row = jnp.concatenate([wo[r, k] for k in range(per_row)], axis=1)
        grad_hidden = (dot_nt(y_row, w_row) * slope[r]).astype(BF16)
        grad[r] = grad_hidden
        terms = dot_nt(grad_hidden, wi[r].reshape(per_row * width, width))
        for k in range(per_row):
            c = where[0, r * per_row + k]
            total[c] = total[c] + terms[:, k * width : (k + 1) * width]
    stores = []
    slab = blocks // SLABS
    for s in range(SLABS):
        at = pl.ds(s * slab, slab)
        rounded[at] = total[at].astype(BF16)
        stores.append(pltpu.make_async_copy(rounded.at[at], placed.at[at], out_sem.at[s]))
        stores[-1].start()
    for copy in stores:
        copy.wait()


def weight_kernel(where, xy, act, grad, own, other, x, y, in_sem):
    load_x, load_y = start_loads(xy, x, y, in_sem)
    for copy in load_x + load_y:
        copy.wait()
    xs, _, rows, each, width, _ = own.shape
    per_row = xs * 2 * each
    core = where[2, 0]
    for r in range(rows):
        act_t = act[r].T
        grad_r = grad[r]
        for x_at in range(xs):
            for half, out in ((core, own), (1 - core, other)):
                for j in range(each):
                    at = r * per_row + (x_at * 2 + half) * each + j
                    out[x_at, 0, r, j] = dot_tn(x[where[0, at]], grad_r).astype(BF16)
                    out[x_at, 1, r, j] = dot_nn(act_t, y[where[1, at]]).astype(BF16)


def per_device(sizes, inputs, upstream, w_in, cols_in, w_out, cols_out):
    nx, nc, ny, nz = sizes
    tok, width = inputs.shape
    rows, per_row = cols_in.shape
    each = per_row // (nx * nc)
    blocks = ny * nz
    smem = pl.BlockSpec(memory_space=pltpu.SMEM)
    vmem = pl.BlockSpec(memory_space=pltpu.VMEM)
    hbm = pl.BlockSpec(memory_space=pltpu.HBM)
    params = pltpu.CompilerParams(vmem_limit_bytes=VMEM_LIMIT)

    where = jnp.stack(
        [
            cols_in.reshape(-1),
            cols_out.reshape(-1),
            jnp.full((rows * per_row,), lax.axis_index("c"), jnp.int32),
        ]
    )
    xy = lax.all_gather(jnp.stack([inputs, upstream]), ("y", "z"), axis=0, tiled=False)
    xy, w_in, w_out = (pltpu.with_memory_space_constraint(v, pltpu.HBM) for v in (xy, w_in, w_out))
    placed, act, grad = pl.pallas_call(
        act_kernel,
        out_shape=(
            jax.ShapeDtypeStruct((blocks, tok, width), BF16),
            jax.ShapeDtypeStruct((rows, tok, width), BF16),
            jax.ShapeDtypeStruct((rows, tok, width), BF16),
        ),
        in_specs=[smem, hbm, hbm, hbm],
        out_specs=(hbm, vmem, vmem),
        scratch_shapes=[
            pltpu.VMEM((blocks, tok, width), BF16),
            pltpu.VMEM((blocks, tok, width), BF16),
            pltpu.VMEM(w_in.shape, BF16),
            pltpu.VMEM(w_out.shape, BF16),
            pltpu.VMEM((blocks, tok, width), F32),
            pltpu.VMEM((blocks, tok, width), BF16),
            pltpu.VMEM((rows, tok, width), F32),
            pltpu.SemaphoreType.DMA((2 * SLABS,)),
            pltpu.SemaphoreType.DMA((2,)),
            pltpu.SemaphoreType.DMA((SLABS,)),
        ],
        compiler_params=params,
        name="act",
    )(where, xy, w_in, w_out)

    over_y = lax.psum_scatter(
        placed.reshape(ny, nz * tok, width), "y", scatter_dimension=0, tiled=False
    )

    half = jax.ShapeDtypeStruct((nx, 2, rows, each, width, width), BF16)
    own, other = pl.pallas_call(
        weight_kernel,
        out_shape=(half, half),
        in_specs=[smem, hbm, vmem, vmem],
        out_specs=(vmem, vmem),
        scratch_shapes=[
            pltpu.VMEM((blocks, tok, width), BF16),
            pltpu.VMEM((blocks, tok, width), BF16),
            pltpu.SemaphoreType.DMA((2 * SLABS,)),
        ],
        compiler_params=params,
        name="weights",
    )(where, xy, act, grad)
    swapped = lax.ppermute(other, "c", [(0, 1), (1, 0)])
    paired = (own.astype(F32) + swapped.astype(F32)).astype(BF16)
    spread = lax.all_to_all(paired, "x", split_axis=0, concat_axis=0, tiled=True)

    over_y, spread = lax.optimization_barrier((over_y, spread))
    over_y = over_y.reshape(nz, tok, width)
    received = lax.all_to_all(over_y, "z", split_axis=0, concat_axis=0, tiled=True)
    summed = jnp.sum(spread.astype(F32), axis=0).astype(BF16)
    grad_inputs = jnp.sum(received.astype(F32), axis=0).astype(BF16)
    return grad_inputs, summed[0], summed[1]


def solution(mesh):
    n_dp, n_blk = mesh.devices.shape
    sizes = (n_dp // 2, 2, 8, n_blk // 8)
    fine = Mesh(mesh.devices.reshape(sizes), ("x", "c", "y", "z"))
    dp, blk = ("x", "c"), ("y", "z")
    return jax.shard_map(
        functools.partial(per_device, sizes),
        mesh=fine,
        in_specs=(
            P(dp, blk),
            P(dp, blk),
            P(blk, None, None, None),
            P(blk, None),
            P(blk, None, None, None),
            P(blk, None),
        ),
        out_specs=(P(dp, blk), P(blk, dp, None, None), P(blk, dp, None, None)),
        check_vma=False,
    )
```

```python
import functools

import jax
import jax.numpy as jnp
from jax import lax
from jax.experimental import pallas as pl
from jax.experimental.pallas import tpu as pltpu
from jax.sharding import Mesh, PartitionSpec as P

BF16 = jnp.bfloat16
F32 = jnp.float32
GELU_SCALE = 0.7978845608028654
GELU_CUBE = 0.044715
VMEM_LIMIT = 52 * 1024 * 1024
SLABS = 8
CYZ = ("c", "y", "z")


def dot_nn(a, b):
    return lax.dot_general(a, b, (((1,), (0,)), ((), ())), preferred_element_type=F32)


def dot_nt(a, b):
    return lax.dot_general(a, b, (((1,), (1,)), ((), ())), preferred_element_type=F32)


def dot_tn(a, b):
    return lax.dot_general(a, b, (((0,), (0,)), ((), ())), preferred_element_type=F32)


def start_loads(where, units, x, y, sem, side):
    places = x.shape[0] // side
    both = []
    for which, into in ((0, x), (1, y)):
        both.append([])
        for n, (ref, steps, first) in enumerate(units):
            place = lax.rem(where[2, 1] + (steps + places), places)
            at = pl.ds(place * side + first, ref.shape[0])
            both[-1].append(
                pltpu.make_async_copy(ref.at[:, which], into.at[at], sem.at[which * len(units) + n])
            )
            both[-1][-1].start()
    return both


def act_kernel(plan, where, *refs):
    side, steps = plan
    units = [(ref, *step) for ref, step in zip(refs, steps)]
    (
        w_in, w_out, placed, act, grad,
        x, y, wi, wo, total, rounded, slope, in_sem, w_sem, out_sem,
    ) = refs[len(steps) :]
    rows, per_row, width, _ = w_in.shape
    blocks = total.shape[0]
    load_in = pltpu.make_async_copy(w_in, wi, w_sem.at[0])
    load_out = pltpu.make_async_copy(w_out, wo, w_sem.at[1])
    load_in.start()
    load_x, load_y = start_loads(where, units, x, y, in_sem, side)
    load_out.start()
    total[...] = jnp.zeros_like(total)
    load_in.wait()
    for copy in load_x:
        copy.wait()
    for r in range(rows):
        x_row = jnp.concatenate([x[where[0, r * per_row + k]] for k in range(per_row)], axis=1)
        hidden = dot_nn(x_row, wi[r].reshape(per_row * width, width))
        square = hidden * hidden
        tanh = jnp.tanh(GELU_SCALE * hidden * (1.0 + GELU_CUBE * square))
        half = 0.5 * (1.0 + tanh)
        act[r] = (hidden * half).astype(BF16)
        slope[r] = half + 0.5 * hidden * (1.0 - tanh * tanh) * (
            GELU_SCALE * (1.0 + 3.0 * GELU_CUBE * square)
        )
    for copy in load_y:
        copy.wait()
    load_out.wait()
    for r in range(rows):
        y_row = jnp.concatenate([y[where[1, r * per_row + k]] for k in range(per_row)], axis=1)
        w_row = jnp.concatenate([wo[r, k] for k in range(per_row)], axis=1)
        grad_hidden = (dot_nt(y_row, w_row) * slope[r]).astype(BF16)
        grad[r] = grad_hidden
        terms = dot_nt(grad_hidden, wi[r].reshape(per_row * width, width))
        for k in range(per_row):
            c = where[0, r * per_row + k]
            total[c] = total[c] + terms[:, k * width : (k + 1) * width]
    stores = []
    slab = blocks // SLABS
    for s in range(SLABS):
        at = pl.ds(s * slab, slab)
        rounded[at] = total[at].astype(BF16)
        stores.append(pltpu.make_async_copy(rounded.at[at], placed.at[at], out_sem.at[s]))
        stores[-1].start()
    for copy in stores:
        copy.wait()


def weight_kernel(plan, where, *refs):
    side, steps = plan
    units = [(ref, *step) for ref, step in zip(refs, steps)]
    act, grad, own, other, x, y, in_sem = refs[len(steps) :]
    load_x, load_y = start_loads(where, units, x, y, in_sem, side)
    for copy in load_x + load_y:
        copy.wait()
    xs, _, rows, each, width, _ = own.shape
    per_row = xs * 2 * each
    core = where[2, 0]
    for r in range(rows):
        act_t = act[r].T
        grad_r = grad[r]
        for away in range(xs):
            x_at = lax.rem(where[2, 2] + away, xs)
            for half, out in ((core, own), (1 - core, other)):
                for j in range(each):
                    at = r * per_row + (x_at * 2 + half) * each + j
                    out[away, 0, r, j] = dot_tn(x[where[0, at]], grad_r).astype(BF16)
                    out[away, 1, r, j] = dot_nn(act_t, y[where[1, at]]).astype(BF16)


def lines_and_rings(ny, nz):
    along_z = [[y * nz + z for z in range(nz)] for y in range(ny)]
    along_y = [[y * nz + z for y in range(ny)] for z in range(nz)]
    second = [[[ny * nz + p for p in group] for group in groups] for groups in (along_z, along_y)]
    return along_z + second[1], along_y + second[0]


def per_device(sizes, inputs, upstream, w_in, cols_in, w_out, cols_out):
    nx, nc, ny, nz = sizes
    side = nz
    tok, width = inputs.shape
    rows, per_row = cols_in.shape
    each = per_row // (nx * nc)
    blocks = ny * nz
    lines, rings = lines_and_rings(ny, nz)
    smem = pl.BlockSpec(memory_space=pltpu.SMEM)
    vmem = pl.BlockSpec(memory_space=pltpu.VMEM)
    anywhere = pl.BlockSpec(memory_space=pl.ANY)
    params = pltpu.CompilerParams(vmem_limit_bytes=VMEM_LIMIT)

    def in_hbm(values):
        return pltpu.with_memory_space_constraint(values, pltpu.HBM)

    def swap(values, groups):
        return lax.all_to_all(
            values, CYZ, split_axis=0, concat_axis=0, tiled=True, axis_index_groups=groups
        )

    def turn(values, by):
        pairs = [(g[i], g[(i + by) % side]) for g in rings for i in range(side)]
        return lax.ppermute(values, CYZ, pairs)

    mine = jnp.stack([inputs, upstream])
    unit = swap(jnp.broadcast_to(mine, (side, *mine.shape)), lines)
    units, steps = [unit], [(0, 0)]
    ahead = back = unit
    for s in range(1, side // 2):
        ahead, back = turn(ahead, 1), turn(back, -1)
        units += [ahead, back]
        steps += [(-s, 0), (s, 0)]
    units += [turn(ahead[: side // 2], 1), turn(back[side // 2 :], -1)]
    steps += [(side // 2, 0), (side // 2, side // 2)]
    units = [in_hbm(u) for u in units]
    plan = (side, tuple(steps))

    core, y_at, z_at = (lax.axis_index(a) for a in CYZ)
    cols = jnp.stack([cols_in.reshape(-1), cols_out.reshape(-1)])
    cols = jnp.where(core == 0, cols, cols % nz * ny + cols // nz)
    place = jnp.where(core == 0, y_at, z_at)
    here = jnp.stack([core, place, lax.axis_index("x")]).astype(jnp.int32)
    here = jnp.pad(here, (0, rows * per_row - 3)).reshape(1, -1)
    where = jnp.concatenate([cols, here])

    gathered = [pltpu.VMEM((blocks, tok, width), BF16)] * 2
    placed, act, grad = pl.pallas_call(
        functools.partial(act_kernel, plan),
        out_shape=(
            jax.ShapeDtypeStruct((blocks, tok, width), BF16),
            jax.ShapeDtypeStruct((rows, tok, width), BF16),
            jax.ShapeDtypeStruct((rows, tok, width), BF16),
        ),
        in_specs=[smem] + [anywhere] * (len(units) + 2),
        out_specs=(anywhere, vmem, vmem),
        scratch_shapes=gathered
        + [
            pltpu.VMEM(w_in.shape, BF16),
            pltpu.VMEM(w_out.shape, BF16),
            pltpu.VMEM((blocks, tok, width), F32),
            pltpu.VMEM((blocks, tok, width), BF16),
            pltpu.VMEM((rows, tok, width), F32),
            pltpu.SemaphoreType.DMA((2 * len(units),)),
            pltpu.SemaphoreType.DMA((2,)),
            pltpu.SemaphoreType.DMA((SLABS,)),
        ],
        compiler_params=params,
        name="act",
    )(where, *units, in_hbm(w_in), in_hbm(w_out))

    on_ring = swap(placed.reshape(side, blocks // side, tok, width), rings)

    half = jax.ShapeDtypeStruct((nx, 2, rows, each, width, width), BF16)
    own, other = pl.pallas_call(
        functools.partial(weight_kernel, plan),
        out_shape=(half, half),
        in_specs=[smem] + [anywhere] * len(units) + [vmem, vmem],
        out_specs=(vmem, vmem),
        scratch_shapes=gathered + [pltpu.SemaphoreType.DMA((2 * len(units),))],
        compiler_params=params,
        name="weights",
    )(where, *units, act, grad)
    swapped = lax.ppermute(other, "c", [(0, 1), (1, 0)])
    paired = [(own[d].astype(F32) + swapped[d].astype(F32)).astype(BF16) for d in range(nx)]
    spread = [
        lax.ppermute(paired[d], "x", [(i, (i + d) % nx) for i in range(nx)]) for d in range(1, nx)
    ]
    summed = sum((v.astype(F32) for v in spread), paired[0].astype(F32)).astype(BF16)

    on_line = jnp.sum(on_ring.astype(F32), axis=0).astype(BF16)
    received = swap(on_line, lines)
    grad_inputs = jnp.sum(received.astype(F32), axis=0).astype(BF16)
    return grad_inputs, summed[0], summed[1]


def solution(mesh):
    n_dp, n_blk = mesh.devices.shape
    sizes = (n_dp // 2, 2, 8, n_blk // 8)
    fine = Mesh(mesh.devices.reshape(sizes), ("x", "c", "y", "z"))
    dp, blk = ("x", "c"), ("y", "z")
    return jax.shard_map(
        functools.partial(per_device, sizes),
        mesh=fine,
        in_specs=(
            P(dp, blk),
            P(dp, blk),
            P(blk, None, None, None),
            P(blk, None),
            P(blk, None, None, None),
            P(blk, None),
        ),
        out_specs=(P(dp, blk), P(blk, dp, None, None), P(blk, dp, None, None)),
        check_vma=False,
    )
```

```python
import functools

import jax
import jax.numpy as jnp
from jax import lax
from jax.experimental import pallas as pl
from jax.experimental.pallas import tpu as pltpu
from jax.sharding import Mesh, PartitionSpec as P

BF16 = jnp.bfloat16
F32 = jnp.float32
GELU_SCALE = 0.7978845608028654
GELU_CUBE = 0.044715
VMEM_LIMIT = 36 * 1024 * 1024
SLABS = 8
CYZ = ("c", "y", "z")


def dot_nn(a, b):
    return lax.dot_general(a, b, (((1,), (0,)), ((), ())), preferred_element_type=F32)


def dot_nt(a, b):
    return lax.dot_general(a, b, (((1,), (1,)), ((), ())), preferred_element_type=F32)


def dot_tn(a, b):
    return lax.dot_general(a, b, (((0,), (0,)), ((), ())), preferred_element_type=F32)


def start_loads(where, units, into, sem, side):
    places = into.shape[0] // side
    loads = []
    for n, (ref, steps) in enumerate(units):
        place = lax.rem(where[2, 1] + (steps + places), places)
        loads.append(pltpu.make_async_copy(ref, into.at[pl.ds(place * side, side)], sem.at[n]))
        loads[-1].start()
    return loads


def hidden_kernel(plan, where, *refs):
    side, steps = plan
    units = list(zip(refs, steps))
    w_in, w_out, act, slope, wi, wo, x, sem, w_sem = refs[len(steps) :]
    rows, per_row, width, _ = w_in.shape
    load_in = pltpu.make_async_copy(w_in, wi, w_sem.at[0])
    load_out = pltpu.make_async_copy(w_out, wo, w_sem.at[1])
    load_in.start()
    loads = start_loads(where, units, x, sem, side)
    load_out.start()
    load_in.wait()
    for copy in loads:
        copy.wait()
    for r in range(rows):
        x_row = jnp.concatenate([x[where[0, r * per_row + k]] for k in range(per_row)], axis=1)
        hidden = dot_nn(x_row, wi[r].reshape(per_row * width, width))
        square = hidden * hidden
        tanh = jnp.tanh(GELU_SCALE * hidden * (1.0 + GELU_CUBE * square))
        half = 0.5 * (1.0 + tanh)
        act[r] = (hidden * half).astype(BF16)
        slope[r] = half + 0.5 * hidden * (1.0 - tanh * tanh) * (
            GELU_SCALE * (1.0 + 3.0 * GELU_CUBE * square)
        )
    load_out.wait()


def back_kernel(plan, where, *refs):
    side, steps = plan
    units = list(zip(refs, steps))
    slope, wi, wo, placed, grad, y, total, rounded, sem, out_sem = refs[len(steps) :]
    rows, per_row, width, _ = wi.shape
    blocks = total.shape[0]
    loads = start_loads(where, units, y, sem, side)
    total[...] = jnp.zeros_like(total)
    for copy in loads:
        copy.wait()
    for r in range(rows):
        y_row = jnp.concatenate([y[where[1, r * per_row + k]] for k in range(per_row)], axis=1)
        w_row = jnp.concatenate([wo[r, k] for k in range(per_row)], axis=1)
        grad_hidden = (dot_nt(y_row, w_row) * slope[r]).astype(BF16)
        grad[r] = grad_hidden
        terms = dot_nt(grad_hidden, wi[r].reshape(per_row * width, width))
        for k in range(per_row):
            c = where[0, r * per_row + k]
            total[c] = total[c] + terms[:, k * width : (k + 1) * width]
    stores = []
    slab = blocks // SLABS
    for s in range(SLABS):
        at = pl.ds(s * slab, slab)
        rounded[at] = total[at].astype(BF16)
        stores.append(pltpu.make_async_copy(rounded.at[at], placed.at[at], out_sem.at[s]))
        stores[-1].start()
    for copy in stores:
        copy.wait()


def weight_kernel(plans, where, *refs):
    (side, x_steps), (_, y_steps) = plans
    n_x, n_y = len(x_steps), len(y_steps)
    act, grad, own, other, x, y, x_sem, y_sem = refs[n_x + n_y :]
    loads = start_loads(where, list(zip(refs[:n_x], x_steps)), x, x_sem, side)
    loads += start_loads(where, list(zip(refs[n_x : n_x + n_y], y_steps)), y, y_sem, side)
    for copy in loads:
        copy.wait()
    xs, _, rows, each, width, _ = own.shape
    per_row = xs * 2 * each
    core = where[2, 0]
    for r in range(rows):
        act_t = act[r].T
        grad_r = grad[r]
        for away in range(xs):
            x_at = lax.rem(where[2, 2] + away, xs)
            for half, out in ((core, own), (1 - core, other)):
                for j in range(each):
                    at = r * per_row + (x_at * 2 + half) * each + j
                    out[away, 0, r, j] = dot_tn(x[where[0, at]], grad_r).astype(BF16)
                    out[away, 1, r, j] = dot_nn(act_t, y[where[1, at]]).astype(BF16)


def lines_and_rings(ny, nz):
    along_z = [[y * nz + z for z in range(nz)] for y in range(ny)]
    along_y = [[y * nz + z for y in range(ny)] for z in range(nz)]
    second = [[[ny * nz + p for p in group] for group in groups] for groups in (along_z, along_y)]
    return along_z + second[1], along_y + second[0]


def per_device(sizes, inputs, upstream, w_in, cols_in, w_out, cols_out):
    nx, nc, ny, nz = sizes
    side = nz
    tok, width = inputs.shape
    rows, per_row = cols_in.shape
    each = per_row // (nx * nc)
    blocks = ny * nz
    lines, rings = lines_and_rings(ny, nz)
    smem = pl.BlockSpec(memory_space=pltpu.SMEM)
    vmem = pl.BlockSpec(memory_space=pltpu.VMEM)
    anywhere = pl.BlockSpec(memory_space=pl.ANY)
    params = pltpu.CompilerParams(vmem_limit_bytes=VMEM_LIMIT)

    def in_hbm(values):
        return pltpu.with_memory_space_constraint(values, pltpu.HBM)

    def swap(values, groups):
        return lax.all_to_all(
            values, CYZ, split_axis=0, concat_axis=0, tiled=True, axis_index_groups=groups
        )

    def turn(values, by):
        pairs = [(g[i], g[(i + by) % side]) for g in rings for i in range(side)]
        return lax.ppermute(values, CYZ, pairs)

    mine = jnp.stack([inputs, upstream])
    unit = swap(jnp.broadcast_to(mine, (side, *mine.shape)), lines)
    x_units, y_units = [unit[:, 0]], [unit[:, 1]]
    x_steps, y_steps = [0], [0]
    x_ahead = x_back = x_units[0]
    y_ahead = y_back = y_units[0]
    for s in range(1, side // 2):
        x_ahead, x_back = turn(x_ahead, 1), turn(x_back, -1)
        y_back, y_ahead = turn(y_back, -1), turn(y_ahead, 1)
        x_units += [x_ahead, x_back]
        y_units += [y_ahead, y_back]
        x_steps += [-s, s]
        y_steps += [-s, s]
    x_units.append(turn(x_ahead, 1))
    y_units.append(turn(y_back, -1))
    x_steps.append(-(side // 2))
    y_steps.append(side // 2)
    x_units, y_units = [in_hbm(u) for u in x_units], [in_hbm(u) for u in y_units]
    x_plan, y_plan = (side, tuple(x_steps)), (side, tuple(y_steps))

    core, y_at, z_at = (lax.axis_index(a) for a in CYZ)
    cols = jnp.stack([cols_in.reshape(-1), cols_out.reshape(-1)])
    cols = jnp.where(core == 0, cols, cols % nz * ny + cols // nz)
    place = jnp.where(core == 0, y_at, z_at)
    here = jnp.stack([core, place, lax.axis_index("x")]).astype(jnp.int32)
    here = jnp.pad(here, (0, rows * per_row - 3)).reshape(1, -1)
    where = jnp.concatenate([cols, here])

    gathered = pltpu.VMEM((blocks, tok, width), BF16)
    loaded = pltpu.SemaphoreType.DMA((side,))
    values = jax.ShapeDtypeStruct((rows, tok, width), BF16)
    act, slope, wi, wo = pl.pallas_call(
        functools.partial(hidden_kernel, x_plan),
        out_shape=(
            values,
            jax.ShapeDtypeStruct((rows, tok, width), F32),
            pltpu.VMEM(w_in.shape, BF16),
            pltpu.VMEM(w_out.shape, BF16),
        ),
        in_specs=[smem] + [anywhere] * (len(x_units) + 2),
        scratch_shapes=[gathered, loaded, pltpu.SemaphoreType.DMA((2,))],
        compiler_params=params,
        name="hidden",
    )(where, *x_units, in_hbm(w_in), in_hbm(w_out))
    placed, grad = pl.pallas_call(
        functools.partial(back_kernel, y_plan),
        out_shape=(jax.ShapeDtypeStruct((blocks, tok, width), BF16), values),
        in_specs=[smem] + [anywhere] * len(y_units) + [vmem] * 3,
        out_specs=(anywhere, vmem),
        scratch_shapes=[
            gathered,
            pltpu.VMEM((blocks, tok, width), F32),
            pltpu.VMEM((blocks, tok, width), BF16),
            loaded,
            pltpu.SemaphoreType.DMA((SLABS,)),
        ],
        compiler_params=params,
        name="back",
    )(where, *y_units, slope, wi, wo)

    on_ring = swap(placed.reshape(side, blocks // side, tok, width), rings)

    half = jax.ShapeDtypeStruct((nx, 2, rows, each, width, width), BF16)
    own, other = pl.pallas_call(
        functools.partial(weight_kernel, (x_plan, y_plan)),
        out_shape=(half, half),
        in_specs=[smem] + [anywhere] * (len(x_units) + len(y_units)) + [vmem, vmem],
        out_specs=(vmem, vmem),
        scratch_shapes=[gathered, gathered, loaded, loaded],
        compiler_params=params,
        name="weights",
    )(where, *x_units, *y_units, act, grad)
    swapped = lax.ppermute(other, "c", [(0, 1), (1, 0)])
    paired = [(own[d].astype(F32) + swapped[d].astype(F32)).astype(BF16) for d in range(nx)]
    spread = [
        lax.ppermute(paired[d], "x", [(i, (i + d) % nx) for i in range(nx)]) for d in range(1, nx)
    ]
    summed = sum((v.astype(F32) for v in spread), paired[0].astype(F32)).astype(BF16)

    on_line = jnp.sum(on_ring.astype(F32), axis=0).astype(BF16)
    received = swap(on_line, lines)
    grad_inputs = jnp.sum(received.astype(F32), axis=0).astype(BF16)
    return grad_inputs, summed[0], summed[1]


def solution(mesh):
    n_dp, n_blk = mesh.devices.shape
    sizes = (n_dp // 2, 2, 8, n_blk // 8)
    fine = Mesh(mesh.devices.reshape(sizes), ("x", "c", "y", "z"))
    dp, blk = ("x", "c"), ("y", "z")
    return jax.shard_map(
        functools.partial(per_device, sizes),
        mesh=fine,
        in_specs=(
            P(dp, blk),
            P(dp, blk),
            P(blk, None, None, None),
            P(blk, None),
            P(blk, None, None, None),
            P(blk, None),
        ),
        out_specs=(P(dp, blk), P(blk, dp, None, None), P(blk, dp, None, None)),
        check_vma=False,
    )
```

```python
import functools

import jax
import jax.numpy as jnp
from jax import lax
from jax.experimental import pallas as pl
from jax.experimental.pallas import tpu as pltpu
from jax.sharding import Mesh, PartitionSpec as P

BF16 = jnp.bfloat16
F32 = jnp.float32
GELU_SCALE = 0.7978845608028654
GELU_CUBE = 0.044715
VMEM_LIMIT = 36 * 1024 * 1024
SLABS = 8
CYZ = ("c", "y", "z")


def dot_nn(a, b):
    return lax.dot_general(a, b, (((1,), (0,)), ((), ())), preferred_element_type=F32)


def dot_nt(a, b):
    return lax.dot_general(a, b, (((1,), (1,)), ((), ())), preferred_element_type=F32)


def dot_tn(a, b):
    return lax.dot_general(a, b, (((0,), (0,)), ((), ())), preferred_element_type=F32)


def start_loads(where, units, into, sem, side):
    places = into.shape[0] // side
    loads = []
    for n, (ref, steps) in enumerate(units):
        place = lax.rem(where[2, 1] + (steps + places), places)
        loads.append(pltpu.make_async_copy(ref, into.at[pl.ds(place * side, side)], sem.at[n]))
        loads[-1].start()
    return loads


def row_of(blocks, where, line, r, per_row):
    return jnp.concatenate([blocks[where[line, r * per_row + k]] for k in range(per_row)], axis=1)


def early_kernel(plans, where, *refs):
    (side, x_steps), (_, y_steps) = plans
    n_x, n_y = len(x_steps), len(y_steps)
    x_units = list(zip(refs[:n_x], x_steps))
    y_units = list(zip(refs[n_x : n_x + n_y], y_steps))
    w_in, w_out, hidden, grad_act, wi, wo, x, y, x_sem, y_sem, w_sem = refs[n_x + n_y :]
    rows, per_row, width, _ = w_in.shape
    load_in = pltpu.make_async_copy(w_in, wi, w_sem.at[0])
    load_out = pltpu.make_async_copy(w_out, wo, w_sem.at[1])
    load_in.start()
    x_loads = start_loads(where, x_units, x, x_sem, side)
    load_out.start()
    y_loads = start_loads(where, y_units, y, y_sem, side)
    places = x.shape[0] // side
    opposite = pl.ds(lax.rem(where[2, 1] + places // 2, places) * side, side)
    x[opposite] = jnp.zeros((side, *x.shape[1:]), BF16)
    y[opposite] = jnp.zeros((side, *y.shape[1:]), BF16)
    load_in.wait()
    for copy in x_loads:
        copy.wait()
    for r in range(rows):
        x_row = row_of(x, where, 0, r, per_row)
        hidden[r] = dot_nn(x_row, wi[r].reshape(per_row * width, width))
    load_out.wait()
    for copy in y_loads:
        copy.wait()
    for r in range(rows):
        w_row = jnp.concatenate([wo[r, k] for k in range(per_row)], axis=1)
        grad_act[r] = dot_nt(row_of(y, where, 1, r, per_row), w_row)


def back_kernel(where, x_last, y_last, hidden_most, grad_most, wi, wo, *refs):
    placed, act, grad, x, y, total, rounded, sem, out_sem = refs
    rows, per_row, width, _ = wi.shape
    blocks, side = total.shape[0], x_last.shape[0]
    load_x = pltpu.make_async_copy(x_last, x.at[pl.ds(0, side)], sem.at[0])
    load_y = pltpu.make_async_copy(y_last, y.at[pl.ds(0, side)], sem.at[1])
    load_x.start()
    load_y.start()
    x[side] = jnp.zeros(x.shape[1:], BF16)
    y[side] = jnp.zeros(y.shape[1:], BF16)
    total[...] = jnp.zeros_like(total)
    load_x.wait()
    load_y.wait()
    for r in range(rows):
        x_row = row_of(x, where, 3, r, per_row)
        y_row = row_of(y, where, 4, r, per_row)
        w_row = jnp.concatenate([wo[r, k] for k in range(per_row)], axis=1)
        hidden = hidden_most[r] + dot_nn(x_row, wi[r].reshape(per_row * width, width))
        grad_act = grad_most[r] + dot_nt(y_row, w_row)
        square = hidden * hidden
        tanh = jnp.tanh(GELU_SCALE * hidden * (1.0 + GELU_CUBE * square))
        half = 0.5 * (1.0 + tanh)
        act[r] = (hidden * half).astype(BF16)
        slope = half + 0.5 * hidden * (1.0 - tanh * tanh) * (
            GELU_SCALE * (1.0 + 3.0 * GELU_CUBE * square)
        )
        grad_hidden = (grad_act * slope).astype(BF16)
        grad[r] = grad_hidden
        terms = dot_nt(grad_hidden, wi[r].reshape(per_row * width, width))
        for k in range(per_row):
            c = where[0, r * per_row + k]
            total[c] = total[c] + terms[:, k * width : (k + 1) * width]
    stores = []
    slab = blocks // SLABS
    for s in range(SLABS):
        at = pl.ds(s * slab, slab)
        rounded[at] = total[at].astype(BF16)
        stores.append(pltpu.make_async_copy(rounded.at[at], placed.at[at], out_sem.at[s]))
        stores[-1].start()
    for copy in stores:
        copy.wait()


def weight_kernel(plans, where, *refs):
    (side, x_steps), (_, y_steps) = plans
    n_x, n_y = len(x_steps), len(y_steps)
    act, grad, own, other, x, y, x_sem, y_sem = refs[n_x + n_y :]
    loads = start_loads(where, list(zip(refs[:n_x], x_steps)), x, x_sem, side)
    loads += start_loads(where, list(zip(refs[n_x : n_x + n_y], y_steps)), y, y_sem, side)
    for copy in loads:
        copy.wait()
    xs, _, rows, each, width, _ = own.shape
    per_row = xs * 2 * each
    core = where[2, 0]
    for r in range(rows):
        act_t = act[r].T
        grad_r = grad[r]
        for away in range(xs):
            x_at = lax.rem(where[2, 2] + away, xs)
            for half, out in ((core, own), (1 - core, other)):
                for j in range(each):
                    at = r * per_row + (x_at * 2 + half) * each + j
                    out[away, 0, r, j] = dot_tn(x[where[0, at]], grad_r).astype(BF16)
                    out[away, 1, r, j] = dot_nn(act_t, y[where[1, at]]).astype(BF16)


def sum_kernel(parts, out, here, sem):
    loads = [
        pltpu.make_async_copy(parts.at[:, n], here.at[n], sem.at[n]) for n in range(here.shape[0])
    ]
    for copy in loads:
        copy.start()
    for n, copy in enumerate(loads):
        copy.wait()
        kept = here[n, 0].astype(F32)
        for s in range(1, here.shape[1]):
            kept = kept + here[n, s].astype(F32)
        out[n] = kept.astype(BF16)


def lines_and_rings(ny, nz):
    along_z = [[y * nz + z for z in range(nz)] for y in range(ny)]
    along_y = [[y * nz + z for y in range(ny)] for z in range(nz)]
    second = [[[ny * nz + p for p in group] for group in groups] for groups in (along_z, along_y)]
    return along_z + second[1], along_y + second[0]


def per_device(sizes, inputs, upstream, w_in, cols_in, w_out, cols_out):
    nx, nc, ny, nz = sizes
    side = nz
    tok, width = inputs.shape
    rows, per_row = cols_in.shape
    each = per_row // (nx * nc)
    blocks = ny * nz
    lines, rings = lines_and_rings(ny, nz)
    smem = pl.BlockSpec(memory_space=pltpu.SMEM)
    vmem = pl.BlockSpec(memory_space=pltpu.VMEM)
    anywhere = pl.BlockSpec(memory_space=pl.ANY)
    params = pltpu.CompilerParams(vmem_limit_bytes=VMEM_LIMIT)

    def in_hbm(values):
        return pltpu.with_memory_space_constraint(values, pltpu.HBM)

    def swap(values, groups):
        return lax.all_to_all(
            values, CYZ, split_axis=0, concat_axis=0, tiled=True, axis_index_groups=groups
        )

    def turn(values, by):
        pairs = [(g[i], g[(i + by) % side]) for g in rings for i in range(side)]
        return lax.ppermute(values, CYZ, pairs)

    mine = jnp.stack([inputs, upstream])
    unit = swap(jnp.broadcast_to(mine, (side, *mine.shape)), lines)
    x_units, y_units = [unit[:, 0]], [unit[:, 1]]
    x_steps, y_steps = [0], [0]
    x_ahead = x_back = x_units[0]
    y_ahead = y_back = y_units[0]
    for s in range(1, side // 2):
        x_ahead, x_back = turn(x_ahead, 1), turn(x_back, -1)
        y_back, y_ahead = turn(y_back, -1), turn(y_ahead, 1)
        x_units += [x_ahead, x_back]
        y_units += [y_ahead, y_back]
        x_steps += [-s, s]
        y_steps += [-s, s]
    x_units.append(turn(x_ahead, 1))
    y_units.append(turn(y_back, -1))
    x_steps.append(-(side // 2))
    y_steps.append(side // 2)
    x_units, y_units = ([in_hbm(u) for u in us[:-1]] + us[-1:] for us in (x_units, y_units))
    x_plan, y_plan = (side, tuple(x_steps)), (side, tuple(y_steps))

    core, y_at, z_at = (lax.axis_index(a) for a in CYZ)
    cols = jnp.stack([cols_in.reshape(-1), cols_out.reshape(-1)])
    cols = jnp.where(core == 0, cols, cols % nz * ny + cols // nz)
    place = jnp.where(core == 0, y_at, z_at)
    here = jnp.stack([core, place, lax.axis_index("x")]).astype(jnp.int32)
    here = jnp.pad(here, (0, rows * per_row - 3)).reshape(1, -1)
    opposite = (place + ny // 2) % ny
    lasts = jnp.where(cols // side == opposite, cols % side, side)
    where = jnp.concatenate([cols, here, lasts])

    gathered = pltpu.VMEM((blocks, tok, width), BF16)
    loaded = pltpu.SemaphoreType.DMA((side,))
    values = jax.ShapeDtypeStruct((rows, tok, width), BF16)
    kept = jax.ShapeDtypeStruct((rows, tok, width), F32)
    hidden_most, grad_most, wi, wo = pl.pallas_call(
        functools.partial(early_kernel, ((side, x_plan[1][:-1]), (side, y_plan[1][:-1]))),
        out_shape=(kept, kept, pltpu.VMEM(w_in.shape, BF16), pltpu.VMEM(w_out.shape, BF16)),
        in_specs=[smem] + [anywhere] * (len(x_units) + len(y_units)),
        scratch_shapes=[gathered, gathered, loaded, loaded, pltpu.SemaphoreType.DMA((2,))],
        compiler_params=params,
        name="early",
    )(where, *x_units[:-1], *y_units[:-1], in_hbm(w_in), in_hbm(w_out))
    last = pltpu.VMEM((side + 1, tok, width), BF16)
    placed, act, grad = pl.pallas_call(
        back_kernel,
        out_shape=(jax.ShapeDtypeStruct((blocks, tok, width), BF16), values, values),
        in_specs=[smem] + [anywhere] * 2 + [vmem] * 4,
        out_specs=(anywhere, vmem, vmem),
        scratch_shapes=[
            last,
            last,
            pltpu.VMEM((blocks, tok, width), F32),
            pltpu.VMEM((blocks, tok, width), BF16),
            pltpu.SemaphoreType.DMA((2,)),
            pltpu.SemaphoreType.DMA((SLABS,)),
        ],
        compiler_params=params,
        name="back",
    )(where, x_units[-1], y_units[-1], hidden_most, grad_most, wi, wo)

    on_ring = swap(placed.reshape(side, blocks // side, tok, width), rings)

    half = jax.ShapeDtypeStruct((nx, 2, rows, each, width, width), BF16)
    own, other = pl.pallas_call(
        functools.partial(weight_kernel, (x_plan, y_plan)),
        out_shape=(half, half),
        in_specs=[smem] + [anywhere] * (len(x_units) + len(y_units)) + [vmem, vmem],
        out_specs=(vmem, vmem),
        scratch_shapes=[gathered, gathered, loaded, loaded],
        compiler_params=params,
        name="weights",
    )(where, *x_units, *y_units, act, grad)
    swapped = lax.ppermute(other, "c", [(0, 1), (1, 0)])
    paired = [(own[d].astype(F32) + swapped[d].astype(F32)).astype(BF16) for d in range(nx)]
    spread = [
        lax.ppermute(paired[d], "x", [(i, (i + d) % nx) for i in range(nx)]) for d in range(1, nx)
    ]
    summed = sum((v.astype(F32) for v in spread), paired[0].astype(F32)).astype(BF16)

    on_line = pl.pallas_call(
        sum_kernel,
        out_shape=jax.ShapeDtypeStruct(on_ring.shape[1:], BF16),
        in_specs=[anywhere],
        out_specs=vmem,
        scratch_shapes=[pltpu.VMEM((blocks // side, side, tok, width), BF16), loaded],
        compiler_params=params,
        name="sums",
    )(in_hbm(on_ring))
    received = swap(on_line, lines)
    grad_inputs = jnp.sum(received.astype(F32), axis=0).astype(BF16)
    return grad_inputs, summed[0], summed[1]


def solution(mesh):
    n_dp, n_blk = mesh.devices.shape
    sizes = (n_dp // 2, 2, 8, n_blk // 8)
    fine = Mesh(mesh.devices.reshape(sizes), ("x", "c", "y", "z"))
    dp, blk = ("x", "c"), ("y", "z")
    return jax.shard_map(
        functools.partial(per_device, sizes),
        mesh=fine,
        in_specs=(
            P(dp, blk),
            P(dp, blk),
            P(blk, None, None, None),
            P(blk, None),
            P(blk, None, None, None),
            P(blk, None),
        ),
        out_specs=(P(dp, blk), P(blk, dp, None, None), P(blk, dp, None, None)),
        check_vma=False,
    )
```

```python
import functools

import jax
import jax.numpy as jnp
from jax import lax
from jax.experimental import pallas as pl
from jax.experimental.pallas import tpu as pltpu
from jax.sharding import Mesh, PartitionSpec as P

BF16 = jnp.bfloat16
F32 = jnp.float32
GELU_SCALE = 0.7978845608028654
GELU_CUBE = 0.044715
VMEM_LIMIT = 36 * 1024 * 1024
SLABS = 8
CYZ = ("c", "y", "z")


def dot_nn(a, b):
    return lax.dot_general(a, b, (((1,), (0,)), ((), ())), preferred_element_type=F32)


def dot_nt(a, b):
    return lax.dot_general(a, b, (((1,), (1,)), ((), ())), preferred_element_type=F32)


def dot_tn(a, b):
    return lax.dot_general(a, b, (((0,), (0,)), ((), ())), preferred_element_type=F32)


def start_loads(where, units, into, sem, side):
    places = into.shape[0] // side
    loads = []
    for n, (ref, steps) in enumerate(units):
        place = lax.rem(where[2, 1] + (steps + places), places)
        loads.append(pltpu.make_async_copy(ref, into.at[pl.ds(place * side, side)], sem.at[n]))
        loads[-1].start()
    return loads


def row_of(blocks, where, line, r, per_row):
    return jnp.concatenate([blocks[where[line, r * per_row + k]] for k in range(per_row)], axis=1)


def last_kernel(where, w_in, w_out, in_last, out_last):
    rows, per_row, width, _ = w_in.shape
    in_last[...] = jnp.zeros_like(in_last)
    out_last[...] = jnp.zeros_like(out_last)
    for r in range(rows):
        at = slice(r * width, (r + 1) * width)
        for k in range(per_row):
            in_last[where[3, r * per_row + k], :, at] = w_in[r, k]
            out_last[where[4, r * per_row + k], :, at] = w_out[r, k].T


def early_kernel(plans, where, *refs):
    (side, x_steps), (_, y_steps) = plans
    n_x, n_y = len(x_steps), len(y_steps)
    x_units = list(zip(refs[:n_x], x_steps))
    y_units = list(zip(refs[n_x : n_x + n_y], y_steps))
    w_in, w_out, in_last, out_last = refs[n_x + n_y : n_x + n_y + 4]
    hidden, grad_act, wi, li, lo, wo, x, y, x_sem, y_sem, w_sem = refs[n_x + n_y + 4 :]
    rows, per_row, width, _ = w_in.shape
    load_in = pltpu.make_async_copy(w_in, wi, w_sem.at[0])
    load_out = pltpu.make_async_copy(w_out, wo, w_sem.at[1])
    load_in.start()
    x_loads = start_loads(where, x_units, x, x_sem, side)
    load_out.start()
    y_loads = start_loads(where, y_units, y, y_sem, side)
    lasts = [
        pltpu.make_async_copy(ref.at[pl.ds(0, side)], into, w_sem.at[2 + n])
        for n, (ref, into) in enumerate(((in_last, li), (out_last, lo)))
    ]
    for copy in lasts:
        copy.start()
    places = x.shape[0] // side
    opposite = pl.ds(lax.rem(where[2, 1] + places // 2, places) * side, side)
    x[opposite] = jnp.zeros((side, *x.shape[1:]), BF16)
    y[opposite] = jnp.zeros((side, *y.shape[1:]), BF16)
    load_in.wait()
    for copy in x_loads:
        copy.wait()
    for r in range(rows):
        x_row = row_of(x, where, 0, r, per_row)
        at = slice(r * width, (r + 1) * width)
        hidden[:, at] = dot_nn(x_row, wi[r].reshape(per_row * width, width))
    load_out.wait()
    for copy in y_loads:
        copy.wait()
    for r in range(rows):
        w_row = jnp.concatenate([wo[r, k] for k in range(per_row)], axis=1)
        at = slice(r * width, (r + 1) * width)
        grad_act[:, at] = dot_nt(row_of(y, where, 1, r, per_row), w_row)
    for copy in lasts:
        copy.wait()


def back_kernel(where, x_last, y_last, hidden_most, grad_most, wi, li, lo, *refs):
    placed, act, grad, total, rounded, out_sem = refs
    rows, per_row, width, _ = wi.shape
    blocks, side = total.shape[0], x_last.shape[0]
    total[...] = jnp.zeros_like(total)
    x_unit = jnp.concatenate([x_last[n] for n in range(side)], axis=1)
    y_unit = jnp.concatenate([y_last[n] for n in range(side)], axis=1)
    hidden = hidden_most[...] + dot_nn(x_unit, li[...].reshape(side * width, rows * width))
    grad_act = grad_most[...] + dot_nn(y_unit, lo[...].reshape(side * width, rows * width))
    square = hidden * hidden
    tanh = jnp.tanh(GELU_SCALE * hidden * (1.0 + GELU_CUBE * square))
    half = 0.5 * (1.0 + tanh)
    slope = half + 0.5 * hidden * (1.0 - tanh * tanh) * (
        GELU_SCALE * (1.0 + 3.0 * GELU_CUBE * square)
    )
    activated = (hidden * half).astype(BF16)
    grad_hidden = (grad_act * slope).astype(BF16)
    for r in range(rows):
        at = slice(r * width, (r + 1) * width)
        act[r] = activated[:, at]
        grad[r] = grad_hidden[:, at]
        terms = dot_nt(grad_hidden[:, at], wi[r].reshape(per_row * width, width))
        for k in range(per_row):
            c = where[0, r * per_row + k]
            total[c] = total[c] + terms[:, k * width : (k + 1) * width]
    stores = []
    slab = blocks // SLABS
    for s in range(SLABS):
        at = pl.ds(s * slab, slab)
        rounded[at] = total[at].astype(BF16)
        stores.append(pltpu.make_async_copy(rounded.at[at], placed.at[at], out_sem.at[s]))
        stores[-1].start()
    for copy in stores:
        copy.wait()


def weight_kernel(plans, where, *refs):
    (side, x_steps), (_, y_steps) = plans
    n_x, n_y = len(x_steps), len(y_steps)
    act, grad, own, other, x, y, x_sem, y_sem = refs[n_x + n_y :]
    loads = start_loads(where, list(zip(refs[:n_x], x_steps)), x, x_sem, side)
    loads += start_loads(where, list(zip(refs[n_x : n_x + n_y], y_steps)), y, y_sem, side)
    for copy in loads:
        copy.wait()
    xs, _, rows, each, width, _ = own.shape
    per_row = xs * 2 * each
    core = where[2, 0]
    for r in range(rows):
        act_t = act[r].T
        grad_r = grad[r]
        for away in range(xs):
            x_at = lax.rem(where[2, 2] + away, xs)
            for half, out in ((core, own), (1 - core, other)):
                for j in range(each):
                    at = r * per_row + (x_at * 2 + half) * each + j
                    out[away, 0, r, j] = dot_tn(x[where[0, at]], grad_r).astype(BF16)
                    out[away, 1, r, j] = dot_nn(act_t, y[where[1, at]]).astype(BF16)


def sum_kernel(parts, out, here, sem):
    loads = [
        pltpu.make_async_copy(parts.at[:, n], here.at[n], sem.at[n]) for n in range(here.shape[0])
    ]
    for copy in loads:
        copy.start()
    for n, copy in enumerate(loads):
        copy.wait()
        kept = here[n, 0].astype(F32)
        for s in range(1, here.shape[1]):
            kept = kept + here[n, s].astype(F32)
        out[n] = kept.astype(BF16)


def lines_and_rings(ny, nz):
    along_z = [[y * nz + z for z in range(nz)] for y in range(ny)]
    along_y = [[y * nz + z for y in range(ny)] for z in range(nz)]
    second = [[[ny * nz + p for p in group] for group in groups] for groups in (along_z, along_y)]
    return along_z + second[1], along_y + second[0]


def per_device(sizes, inputs, upstream, w_in, cols_in, w_out, cols_out):
    nx, nc, ny, nz = sizes
    side = nz
    tok, width = inputs.shape
    rows, per_row = cols_in.shape
    each = per_row // (nx * nc)
    blocks = ny * nz
    lines, rings = lines_and_rings(ny, nz)
    smem = pl.BlockSpec(memory_space=pltpu.SMEM)
    vmem = pl.BlockSpec(memory_space=pltpu.VMEM)
    anywhere = pl.BlockSpec(memory_space=pl.ANY)
    params = pltpu.CompilerParams(vmem_limit_bytes=VMEM_LIMIT)

    def in_hbm(values):
        return pltpu.with_memory_space_constraint(values, pltpu.HBM)

    def swap(values, groups):
        return lax.all_to_all(
            values, CYZ, split_axis=0, concat_axis=0, tiled=True, axis_index_groups=groups
        )

    def turn(values, by):
        pairs = [(g[i], g[(i + by) % side]) for g in rings for i in range(side)]
        return lax.ppermute(values, CYZ, pairs)

    core, y_at, z_at = (lax.axis_index(a) for a in CYZ)
    cols = jnp.stack([cols_in.reshape(-1), cols_out.reshape(-1)])
    cols = jnp.where(core == 0, cols, cols % nz * ny + cols // nz)
    place = jnp.where(core == 0, y_at, z_at)
    here = jnp.stack([core, place, lax.axis_index("x")]).astype(jnp.int32)
    here = jnp.pad(here, (0, rows * per_row - 3)).reshape(1, -1)
    opposite = (place + ny // 2) % ny
    lasts = jnp.where(cols // side == opposite, cols % side, side)
    where = jnp.concatenate([cols, here, lasts])

    mine = jnp.stack([inputs, upstream])
    unit = swap(jnp.broadcast_to(mine, (side, *mine.shape)), lines)
    dense = jax.ShapeDtypeStruct((side + 1, width, rows * width), BF16)
    in_last, out_last = pl.pallas_call(
        last_kernel,
        out_shape=(dense, dense),
        in_specs=[smem, vmem, vmem],
        out_specs=(vmem, vmem),
        compiler_params=params,
        name="last",
    )(where, w_in, w_out)
    unit, in_last, out_last = lax.optimization_barrier((unit, in_last, out_last))
    x_units, y_units = [unit[:, 0]], [unit[:, 1]]
    x_steps, y_steps = [0], [0]
    x_ahead = x_back = x_units[0]
    y_ahead = y_back = y_units[0]
    for s in range(1, side // 2):
        x_ahead, x_back = turn(x_ahead, 1), turn(x_back, -1)
        y_back, y_ahead = turn(y_back, -1), turn(y_ahead, 1)
        x_units += [x_ahead, x_back]
        y_units += [y_ahead, y_back]
        x_steps += [-s, s]
        y_steps += [-s, s]
    x_units.append(turn(x_ahead, 1))
    y_units.append(turn(y_back, -1))
    x_steps.append(-(side // 2))
    y_steps.append(side // 2)
    x_units, y_units = ([in_hbm(u) for u in us[:-1]] + us[-1:] for us in (x_units, y_units))
    x_plan, y_plan = (side, tuple(x_steps)), (side, tuple(y_steps))

    gathered = pltpu.VMEM((blocks, tok, width), BF16)
    loaded = pltpu.SemaphoreType.DMA((side,))
    values = jax.ShapeDtypeStruct((rows, tok, width), BF16)
    kept = pltpu.VMEM((tok, rows * width), F32)
    last = pltpu.VMEM((side, width, rows * width), BF16)
    hidden_most, grad_most, wi, li, lo = pl.pallas_call(
        functools.partial(early_kernel, ((side, x_plan[1][:-1]), (side, y_plan[1][:-1]))),
        out_shape=(kept, kept, pltpu.VMEM(w_in.shape, BF16), last, last),
        in_specs=[smem] + [anywhere] * (len(x_units) + len(y_units) + 2),
        scratch_shapes=[
            pltpu.VMEM(w_out.shape, BF16),
            gathered,
            gathered,
            loaded,
            loaded,
            pltpu.SemaphoreType.DMA((4,)),
        ],
        compiler_params=params,
        name="early",
    )(where, *x_units[:-1], *y_units[:-1], *(in_hbm(v) for v in (w_in, w_out, in_last, out_last)))
    placed, act, grad = pl.pallas_call(
        back_kernel,
        out_shape=(jax.ShapeDtypeStruct((blocks, tok, width), BF16), values, values),
        in_specs=[smem] + [vmem] * 7,
        out_specs=(anywhere, vmem, vmem),
        scratch_shapes=[
            pltpu.VMEM((blocks, tok, width), F32),
            pltpu.VMEM((blocks, tok, width), BF16),
            pltpu.SemaphoreType.DMA((SLABS,)),
        ],
        compiler_params=params,
        name="back",
    )(where, x_units[-1], y_units[-1], hidden_most, grad_most, wi, li, lo)

    on_ring = swap(placed.reshape(side, blocks // side, tok, width), rings)

    half = jax.ShapeDtypeStruct((nx, 2, rows, each, width, width), BF16)
    own, other = pl.pallas_call(
        functools.partial(weight_kernel, (x_plan, y_plan)),
        out_shape=(half, half),
        in_specs=[smem] + [anywhere] * (len(x_units) + len(y_units)) + [vmem, vmem],
        out_specs=(vmem, vmem),
        scratch_shapes=[gathered, gathered, loaded, loaded],
        compiler_params=params,
        name="weights",
    )(where, *x_units, *y_units, act, grad)
    swapped = lax.ppermute(other, "c", [(0, 1), (1, 0)])
    paired = [(own[d].astype(F32) + swapped[d].astype(F32)).astype(BF16) for d in range(nx)]
    spread = [
        lax.ppermute(paired[d], "x", [(i, (i + d) % nx) for i in range(nx)]) for d in range(1, nx)
    ]
    summed = sum((v.astype(F32) for v in spread), paired[0].astype(F32)).astype(BF16)

    on_line = pl.pallas_call(
        sum_kernel,
        out_shape=jax.ShapeDtypeStruct(on_ring.shape[1:], BF16),
        in_specs=[anywhere],
        out_specs=vmem,
        scratch_shapes=[pltpu.VMEM((blocks // side, side, tok, width), BF16), loaded],
        compiler_params=params,
        name="sums",
    )(in_hbm(on_ring))
    received = swap(on_line, lines)
    grad_inputs = jnp.sum(received.astype(F32), axis=0).astype(BF16)
    return grad_inputs, summed[0], summed[1]


def solution(mesh):
    n_dp, n_blk = mesh.devices.shape
    sizes = (n_dp // 2, 2, 8, n_blk // 8)
    fine = Mesh(mesh.devices.reshape(sizes), ("x", "c", "y", "z"))
    dp, blk = ("x", "c"), ("y", "z")
    return jax.shard_map(
        functools.partial(per_device, sizes),
        mesh=fine,
        in_specs=(
            P(dp, blk),
            P(dp, blk),
            P(blk, None, None, None),
            P(blk, None),
            P(blk, None, None, None),
            P(blk, None),
        ),
        out_specs=(P(dp, blk), P(blk, dp, None, None), P(blk, dp, None, None)),
        check_vma=False,
    )
```

```python
import functools

import jax
import jax.numpy as jnp
from jax import lax
from jax.experimental import pallas as pl
from jax.experimental.pallas import tpu as pltpu
from jax.sharding import Mesh, PartitionSpec as P

BF16 = jnp.bfloat16
F32 = jnp.float32
GELU_SCALE = 0.7978845608028654
GELU_CUBE = 0.044715
VMEM_LIMIT = 36 * 1024 * 1024
SLABS = 8
CYZ = ("c", "y", "z")


def dot_nn(a, b):
    return lax.dot_general(a, b, (((1,), (0,)), ((), ())), preferred_element_type=F32)


def dot_nt(a, b):
    return lax.dot_general(a, b, (((1,), (1,)), ((), ())), preferred_element_type=F32)


def dot_tn(a, b):
    return lax.dot_general(a, b, (((0,), (0,)), ((), ())), preferred_element_type=F32)


def start_loads(where, units, into, sem, side):
    places = into.shape[0] // side
    loads = []
    for n, (ref, steps) in enumerate(units):
        place = lax.rem(where[2, 1] + (steps + places), places)
        loads.append(pltpu.make_async_copy(ref, into.at[pl.ds(place * side, side)], sem.at[n]))
        loads[-1].start()
    return loads


def row_of(blocks, where, line, r, per_row):
    return jnp.concatenate([blocks[where[line, r * per_row + k]] for k in range(per_row)], axis=1)


def last_kernel(where, w_in, w_out, in_last, out_last):
    rows, per_row, width, _ = w_in.shape
    in_last[...] = jnp.zeros_like(in_last)
    out_last[...] = jnp.zeros_like(out_last)
    for r in range(rows):
        at = slice(r * width, (r + 1) * width)
        for k in range(per_row):
            in_last[where[3, r * per_row + k], :, at] = w_in[r, k]
            out_last[where[4, r * per_row + k], :, at] = w_out[r, k].T


def early_kernel(plans, where, *refs):
    (side, x_steps), (_, y_steps) = plans
    n_x, n_y = len(x_steps), len(y_steps)
    x_units = list(zip(refs[:n_x], x_steps))
    y_units = list(zip(refs[n_x : n_x + n_y], y_steps))
    w_in, w_out, in_last, out_last = refs[n_x + n_y : n_x + n_y + 4]
    hidden, grad_act, wi, li, lo, wo, x, y, x_sem, y_sem, w_sem = refs[n_x + n_y + 4 :]
    rows, per_row, width, _ = w_in.shape
    load_in = pltpu.make_async_copy(w_in, wi, w_sem.at[0])
    load_out = pltpu.make_async_copy(w_out, wo, w_sem.at[1])
    load_in.start()
    x_loads = start_loads(where, x_units, x, x_sem, side)
    load_out.start()
    y_loads = start_loads(where, y_units, y, y_sem, side)
    lasts = [
        pltpu.make_async_copy(ref.at[pl.ds(0, side)], into, w_sem.at[2 + n])
        for n, (ref, into) in enumerate(((in_last, li), (out_last, lo)))
    ]
    for copy in lasts:
        copy.start()
    places = x.shape[0] // side
    opposite = pl.ds(lax.rem(where[2, 1] + places // 2, places) * side, side)
    x[opposite] = jnp.zeros((side, *x.shape[1:]), BF16)
    y[opposite] = jnp.zeros((side, *y.shape[1:]), BF16)
    load_in.wait()
    for copy in x_loads:
        copy.wait()
    for r in range(rows):
        x_row = row_of(x, where, 0, r, per_row)
        at = slice(r * width, (r + 1) * width)
        hidden[:, at] = dot_nn(x_row, wi[r].reshape(per_row * width, width))
    load_out.wait()
    for copy in y_loads:
        copy.wait()
    for r in range(rows):
        w_row = jnp.concatenate([wo[r, k] for k in range(per_row)], axis=1)
        at = slice(r * width, (r + 1) * width)
        grad_act[:, at] = dot_nt(row_of(y, where, 1, r, per_row), w_row)
    for copy in lasts:
        copy.wait()


def back_kernel(where, x_last, y_last, hidden_most, grad_most, wi, li, lo, *refs):
    placed, act_out, grad_out, total, rounded, act, grad, out_sem = refs
    rows, per_row, width, _ = wi.shape
    blocks, side = total.shape[0], x_last.shape[0]
    total[...] = jnp.zeros_like(total)
    x_unit = jnp.concatenate([x_last[n] for n in range(side)], axis=1)
    y_unit = jnp.concatenate([y_last[n] for n in range(side)], axis=1)
    hidden = hidden_most[...] + dot_nn(x_unit, li[...].reshape(side * width, rows * width))
    grad_act = grad_most[...] + dot_nn(y_unit, lo[...].reshape(side * width, rows * width))
    square = hidden * hidden
    tanh = jnp.tanh(GELU_SCALE * hidden * (1.0 + GELU_CUBE * square))
    half = 0.5 * (1.0 + tanh)
    slope = half + 0.5 * hidden * (1.0 - tanh * tanh) * (
        GELU_SCALE * (1.0 + 3.0 * GELU_CUBE * square)
    )
    activated = (hidden * half).astype(BF16)
    grad_hidden = (grad_act * slope).astype(BF16)
    for r in range(rows):
        at = slice(r * width, (r + 1) * width)
        act[r] = activated[:, at]
        grad[r] = grad_hidden[:, at]
    stores = [
        pltpu.make_async_copy(act, act_out, out_sem.at[SLABS]),
        pltpu.make_async_copy(grad, grad_out, out_sem.at[SLABS + 1]),
    ]
    for copy in stores:
        copy.start()
    for r in range(rows):
        at = slice(r * width, (r + 1) * width)
        terms = dot_nt(grad_hidden[:, at], wi[r].reshape(per_row * width, width))
        for k in range(per_row):
            c = where[0, r * per_row + k]
            total[c] = total[c] + terms[:, k * width : (k + 1) * width]
    slab = blocks // SLABS
    for s in range(SLABS):
        at = pl.ds(s * slab, slab)
        rounded[at] = total[at].astype(BF16)
        stores.append(pltpu.make_async_copy(rounded.at[at], placed.at[s], out_sem.at[s]))
        stores[-1].start()
    for copy in stores:
        copy.wait()


def weight_kernel(plans, where, *refs):
    (side, x_steps), (_, y_steps) = plans
    n_x, n_y = len(x_steps), len(y_steps)
    act_in, grad_in, own, other, x, y, act, grad, x_sem, y_sem, sem = refs[n_x + n_y :]
    loads = [
        pltpu.make_async_copy(act_in, act, sem.at[0]),
        pltpu.make_async_copy(grad_in, grad, sem.at[1]),
    ]
    for copy in loads:
        copy.start()
    loads += start_loads(where, list(zip(refs[:n_x], x_steps)), x, x_sem, side)
    loads += start_loads(where, list(zip(refs[n_x : n_x + n_y], y_steps)), y, y_sem, side)
    for copy in loads:
        copy.wait()
    xs, _, rows, each, width, _ = own.shape
    per_row = xs * 2 * each
    core = where[2, 0]
    for r in range(rows):
        act_t = act[r].T
        grad_r = grad[r]
        for away in range(xs):
            x_at = lax.rem(where[2, 2] + away, xs)
            for half, out in ((core, own), (1 - core, other)):
                for j in range(each):
                    at = r * per_row + (x_at * 2 + half) * each + j
                    out[away, 0, r, j] = dot_tn(x[where[0, at]], grad_r).astype(BF16)
                    out[away, 1, r, j] = dot_nn(act_t, y[where[1, at]]).astype(BF16)


def sum_kernel(parts, out):
    for n in range(parts.shape[1]):
        kept = parts[0, n].astype(F32)
        for s in range(1, parts.shape[0]):
            kept = kept + parts[s, n].astype(F32)
        out[n] = kept.astype(BF16)


def lines_and_rings(ny, nz):
    along_z = [[y * nz + z for z in range(nz)] for y in range(ny)]
    along_y = [[y * nz + z for y in range(ny)] for z in range(nz)]
    second = [[[ny * nz + p for p in group] for group in groups] for groups in (along_z, along_y)]
    return along_z + second[1], along_y + second[0]


def per_device(sizes, inputs, upstream, w_in, cols_in, w_out, cols_out):
    nx, nc, ny, nz = sizes
    side = nz
    tok, width = inputs.shape
    rows, per_row = cols_in.shape
    each = per_row // (nx * nc)
    blocks = ny * nz
    lines, rings = lines_and_rings(ny, nz)
    smem = pl.BlockSpec(memory_space=pltpu.SMEM)
    vmem = pl.BlockSpec(memory_space=pltpu.VMEM)
    anywhere = pl.BlockSpec(memory_space=pl.ANY)
    params = pltpu.CompilerParams(vmem_limit_bytes=VMEM_LIMIT)

    def in_hbm(values):
        return pltpu.with_memory_space_constraint(values, pltpu.HBM)

    def swap(values, groups):
        return lax.all_to_all(
            values, CYZ, split_axis=0, concat_axis=0, tiled=True, axis_index_groups=groups
        )

    def turn(values, by):
        pairs = [(g[i], g[(i + by) % side]) for g in rings for i in range(side)]
        return lax.ppermute(values, CYZ, pairs)

    core, y_at, z_at = (lax.axis_index(a) for a in CYZ)
    cols = jnp.stack([cols_in.reshape(-1), cols_out.reshape(-1)])
    cols = jnp.where(core == 0, cols, cols % nz * ny + cols // nz)
    place = jnp.where(core == 0, y_at, z_at)
    here = jnp.stack([core, place, lax.axis_index("x")]).astype(jnp.int32)
    here = jnp.pad(here, (0, rows * per_row - 3)).reshape(1, -1)
    opposite = (place + ny // 2) % ny
    lasts = jnp.where(cols // side == opposite, cols % side, side)
    where = jnp.concatenate([cols, here, lasts])

    which = lax.broadcasted_iota(jnp.int32, (side, 2, tok, width), 1)
    unit = swap(jnp.where(which == 0, inputs, upstream), lines)
    dense = jax.ShapeDtypeStruct((side + 1, width, rows * width), BF16)
    in_last, out_last = pl.pallas_call(
        last_kernel,
        out_shape=(dense, dense),
        in_specs=[smem, vmem, vmem],
        out_specs=(vmem, vmem),
        compiler_params=params,
        name="last",
    )(where, w_in, w_out)
    unit, in_last, out_last = lax.optimization_barrier((unit, in_last, out_last))
    x_units, y_units = [unit[:, 0]], [unit[:, 1]]
    x_steps, y_steps = [0], [0]
    x_ahead = x_back = x_units[0]
    y_ahead = y_back = y_units[0]
    for s in range(1, side // 2):
        x_ahead, x_back = turn(x_ahead, 1), turn(x_back, -1)
        y_back, y_ahead = turn(y_back, -1), turn(y_ahead, 1)
        x_units += [x_ahead, x_back]
        y_units += [y_ahead, y_back]
        x_steps += [-s, s]
        y_steps += [-s, s]
    x_units.append(turn(x_ahead, 1))
    y_units.append(turn(y_back, -1))
    x_steps.append(-(side // 2))
    y_steps.append(side // 2)
    x_units, y_units = ([in_hbm(u) for u in us[:-1]] + us[-1:] for us in (x_units, y_units))
    x_plan, y_plan = (side, tuple(x_steps)), (side, tuple(y_steps))

    gathered = pltpu.VMEM((blocks, tok, width), BF16)
    loaded = pltpu.SemaphoreType.DMA((side,))
    values = pltpu.HBM((rows, tok, width), BF16)
    kept = pltpu.VMEM((tok, rows * width), F32)
    last = pltpu.VMEM((side, width, rows * width), BF16)
    hidden_most, grad_most, wi, li, lo = pl.pallas_call(
        functools.partial(early_kernel, ((side, x_plan[1][:-1]), (side, y_plan[1][:-1]))),
        out_shape=(kept, kept, pltpu.VMEM(w_in.shape, BF16), last, last),
        in_specs=[smem] + [anywhere] * (len(x_units) + len(y_units) + 2),
        scratch_shapes=[
            pltpu.VMEM(w_out.shape, BF16),
            gathered,
            gathered,
            loaded,
            loaded,
            pltpu.SemaphoreType.DMA((4,)),
        ],
        compiler_params=params,
        name="early",
    )(where, *x_units[:-1], *y_units[:-1], *(in_hbm(v) for v in (w_in, w_out, in_last, out_last)))
    placed, act, grad = pl.pallas_call(
        back_kernel,
        out_shape=(pltpu.HBM((side, blocks // side, tok, width), BF16), values, values),
        in_specs=[smem] + [vmem] * 7,
        scratch_shapes=[
            pltpu.VMEM((blocks, tok, width), F32),
            pltpu.VMEM((blocks, tok, width), BF16),
            pltpu.VMEM((rows, tok, width), BF16),
            pltpu.VMEM((rows, tok, width), BF16),
            pltpu.SemaphoreType.DMA((SLABS + 2,)),
        ],
        compiler_params=params,
        name="back",
    )(where, x_units[-1], y_units[-1], hidden_most, grad_most, wi, li, lo)

    on_ring = swap(placed, rings)

    half = jax.ShapeDtypeStruct((nx, 2, rows, each, width, width), BF16)
    own, other = pl.pallas_call(
        functools.partial(weight_kernel, (x_plan, y_plan)),
        out_shape=(half, half),
        in_specs=[smem] + [anywhere] * (len(x_units) + len(y_units) + 2),
        out_specs=(vmem, vmem),
        scratch_shapes=[
            gathered,
            gathered,
            pltpu.VMEM((rows, tok, width), BF16),
            pltpu.VMEM((rows, tok, width), BF16),
            loaded,
            loaded,
            pltpu.SemaphoreType.DMA((2,)),
        ],
        compiler_params=params,
        name="weights",
    )(where, *x_units, *y_units, act, grad)
    swapped = lax.ppermute(other, "c", [(0, 1), (1, 0)])
    paired = [(own[d].astype(F32) + swapped[d].astype(F32)).astype(BF16) for d in range(nx)]
    spread = [
        lax.ppermute(paired[d], "x", [(i, (i + d) % nx) for i in range(nx)]) for d in range(1, nx)
    ]
    summed = sum((v.astype(F32) for v in spread), paired[0].astype(F32)).astype(BF16)

    on_line = pl.pallas_call(
        sum_kernel,
        out_shape=jax.ShapeDtypeStruct(on_ring.shape[1:], BF16),
        in_specs=[vmem],
        out_specs=vmem,
        compiler_params=params,
        name="sums",
    )(pltpu.with_memory_space_constraint(on_ring, pltpu.VMEM))
    received = swap(on_line, lines)
    grad_inputs = jnp.sum(received.astype(F32), axis=0).astype(BF16)
    return grad_inputs, summed[0], summed[1]


def solution(mesh):
    n_dp, n_blk = mesh.devices.shape
    sizes = (n_dp // 2, 2, 8, n_blk // 8)
    fine = Mesh(mesh.devices.reshape(sizes), ("x", "c", "y", "z"))
    dp, blk = ("x", "c"), ("y", "z")
    return jax.shard_map(
        functools.partial(per_device, sizes),
        mesh=fine,
        in_specs=(
            P(dp, blk),
            P(dp, blk),
            P(blk, None, None, None),
            P(blk, None),
            P(blk, None, None, None),
            P(blk, None),
        ),
        out_specs=(P(dp, blk), P(blk, dp, None, None), P(blk, dp, None, None)),
        check_vma=False,
    )
```

```python
import functools

import jax
import jax.numpy as jnp
from jax import lax
from jax.experimental import pallas as pl
from jax.experimental.pallas import tpu as pltpu
from jax.sharding import Mesh, PartitionSpec as P

BF16 = jnp.bfloat16
F32 = jnp.float32
GELU_SCALE = 0.7978845608028654
GELU_CUBE = 0.044715
VMEM_LIMIT = 36 * 1024 * 1024
SLABS = 8
CYZ = ("c", "y", "z")


def dot_nn(a, b):
    return lax.dot_general(a, b, (((1,), (0,)), ((), ())), preferred_element_type=F32)


def dot_nt(a, b):
    return lax.dot_general(a, b, (((1,), (1,)), ((), ())), preferred_element_type=F32)


def dot_tn(a, b):
    return lax.dot_general(a, b, (((0,), (0,)), ((), ())), preferred_element_type=F32)


def start_loads(where, units, into, sem, side):
    places = into.shape[0] // side
    loads = []
    for n, (ref, steps) in enumerate(units):
        place = lax.rem(where[2, 1] + (steps + places), places)
        loads.append(pltpu.make_async_copy(ref, into.at[pl.ds(place * side, side)], sem.at[n]))
        loads[-1].start()
    return loads


def row_of(blocks, where, line, r, per_row):
    return jnp.concatenate([blocks[where[line, r * per_row + k]] for k in range(per_row)], axis=1)


def last_kernel(where, w_in, w_out, in_last, out_last):
    rows, per_row, width, _ = w_in.shape
    in_last[...] = jnp.zeros_like(in_last)
    out_last[...] = jnp.zeros_like(out_last)
    for r in range(rows):
        at = slice(r * width, (r + 1) * width)
        for k in range(per_row):
            in_last[where[3, r * per_row + k], :, at] = w_in[r, k]
            out_last[where[4, r * per_row + k], :, at] = w_out[r, k].T


def early_kernel(plans, where, *refs):
    (side, x_steps), (_, y_steps) = plans
    n_x, n_y = len(x_steps), len(y_steps)
    x_units = list(zip(refs[:n_x], x_steps))
    y_units = list(zip(refs[n_x : n_x + n_y], y_steps))
    w_in, w_out, in_last, out_last = refs[n_x + n_y : n_x + n_y + 4]
    hidden, grad_act, wi, li, lo, wo, x, y, x_sem, y_sem, w_sem = refs[n_x + n_y + 4 :]
    rows, per_row, width, _ = w_in.shape
    load_in = pltpu.make_async_copy(w_in, wi, w_sem.at[0])
    load_out = pltpu.make_async_copy(w_out, wo, w_sem.at[1])
    load_in.start()
    x_loads = start_loads(where, x_units, x, x_sem, side)
    load_out.start()
    y_loads = start_loads(where, y_units, y, y_sem, side)
    lasts = [
        pltpu.make_async_copy(ref.at[pl.ds(0, side)], into, w_sem.at[2 + n])
        for n, (ref, into) in enumerate(((in_last, li), (out_last, lo)))
    ]
    for copy in lasts:
        copy.start()
    places = x.shape[0] // side
    opposite = pl.ds(lax.rem(where[2, 1] + places // 2, places) * side, side)
    x[opposite] = jnp.zeros((side, *x.shape[1:]), BF16)
    y[opposite] = jnp.zeros((side, *y.shape[1:]), BF16)
    load_in.wait()
    for copy in x_loads:
        copy.wait()
    for r in range(rows):
        x_row = row_of(x, where, 0, r, per_row)
        at = slice(r * width, (r + 1) * width)
        hidden[:, at] = dot_nn(x_row, wi[r].reshape(per_row * width, width))
    load_out.wait()
    for copy in y_loads:
        copy.wait()
    for r in range(rows):
        w_row = jnp.concatenate([wo[r, k] for k in range(per_row)], axis=1)
        at = slice(r * width, (r + 1) * width)
        grad_act[:, at] = dot_nt(row_of(y, where, 1, r, per_row), w_row)
    for copy in lasts:
        copy.wait()


def back_kernel(where, x_last, y_last, hidden_most, grad_most, wi, li, lo, *refs):
    placed, act_out, grad_out, total, rounded, act, grad, out_sem = refs
    rows, per_row, width, _ = wi.shape
    blocks, side = total.shape[0], x_last.shape[0]
    total[...] = jnp.zeros_like(total)
    x_unit = jnp.concatenate([x_last[n] for n in range(side)], axis=1)
    y_unit = jnp.concatenate([y_last[n] for n in range(side)], axis=1)
    hidden = hidden_most[...] + dot_nn(x_unit, li[...].reshape(side * width, rows * width))
    grad_act = grad_most[...] + dot_nn(y_unit, lo[...].reshape(side * width, rows * width))
    square = hidden * hidden
    tanh = jnp.tanh(GELU_SCALE * hidden * (1.0 + GELU_CUBE * square))
    half = 0.5 * (1.0 + tanh)
    slope = half + 0.5 * hidden * (1.0 - tanh * tanh) * (
        GELU_SCALE * (1.0 + 3.0 * GELU_CUBE * square)
    )
    activated = (hidden * half).astype(BF16)
    grad_hidden = (grad_act * slope).astype(BF16)
    for r in range(rows):
        at = slice(r * width, (r + 1) * width)
        act[r] = activated[:, at]
        grad[r] = grad_hidden[:, at]
    stores = [
        pltpu.make_async_copy(act, act_out, out_sem.at[SLABS]),
        pltpu.make_async_copy(grad, grad_out, out_sem.at[SLABS + 1]),
    ]
    for copy in stores:
        copy.start()
    for r in range(rows):
        at = slice(r * width, (r + 1) * width)
        terms = dot_nt(grad_hidden[:, at], wi[r].reshape(per_row * width, width))
        for k in range(per_row):
            c = where[0, r * per_row + k]
            total[c] = total[c] + terms[:, k * width : (k + 1) * width]
    slab = blocks // SLABS
    for s in range(SLABS):
        at = pl.ds(s * slab, slab)
        rounded[at] = total[at].astype(BF16)
        stores.append(pltpu.make_async_copy(rounded.at[at], placed.at[s], out_sem.at[s]))
        stores[-1].start()
    for copy in stores:
        copy.wait()


def weight_kernel(plans, where, *refs):
    (side, x_steps), (_, y_steps) = plans
    n_x, n_y = len(x_steps), len(y_steps)
    act_in, grad_in, own, other, x, y, act, grad, x_sem, y_sem, sem = refs[n_x + n_y :]
    loads = [
        pltpu.make_async_copy(act_in, act, sem.at[0]),
        pltpu.make_async_copy(grad_in, grad, sem.at[1]),
    ]
    for copy in loads:
        copy.start()
    loads += start_loads(where, list(zip(refs[:n_x], x_steps)), x, x_sem, side)
    loads += start_loads(where, list(zip(refs[n_x : n_x + n_y], y_steps)), y, y_sem, side)
    for copy in loads:
        copy.wait()
    xs, _, rows, each, width, _ = own.shape
    per_row = xs * 2 * each
    core = where[2, 0]
    for r in range(rows):
        act_t = act[r].T
        grad_r = grad[r]
        for away in range(xs):
            x_at = lax.rem(where[2, 2] + away, xs)
            for half, out in ((core, own), (1 - core, other)):
                for j in range(each):
                    at = r * per_row + (x_at * 2 + half) * each + j
                    out[away, 0, r, j] = dot_tn(x[where[0, at]], grad_r).astype(BF16)
                    out[away, 1, r, j] = dot_nn(act_t, y[where[1, at]]).astype(BF16)


def sum_kernel(parts, out):
    for n in range(parts.shape[1]):
        kept = parts[0, n].astype(F32)
        for s in range(1, parts.shape[0]):
            kept = kept + parts[s, n].astype(F32)
        out[n] = kept.astype(BF16)


def lines_and_rings(ny, nz):
    along_z = [[y * nz + z for z in range(nz)] for y in range(ny)]
    along_y = [[y * nz + z for y in range(ny)] for z in range(nz)]
    second = [[[ny * nz + p for p in group] for group in groups] for groups in (along_z, along_y)]
    return along_z + second[1], along_y + second[0]


def per_device(sizes, inputs, upstream, w_in, cols_in, w_out, cols_out):
    nx, nc, ny, nz = sizes
    side = nz
    tok, width = inputs.shape
    rows, per_row = cols_in.shape
    each = per_row // (nx * nc)
    blocks = ny * nz
    lines, rings = lines_and_rings(ny, nz)
    smem = pl.BlockSpec(memory_space=pltpu.SMEM)
    vmem = pl.BlockSpec(memory_space=pltpu.VMEM)
    anywhere = pl.BlockSpec(memory_space=pl.ANY)
    params = pltpu.CompilerParams(vmem_limit_bytes=VMEM_LIMIT)

    def in_hbm(values):
        return pltpu.with_memory_space_constraint(values, pltpu.HBM)

    def swap(values, groups):
        return lax.all_to_all(
            values, CYZ, split_axis=0, concat_axis=0, tiled=True, axis_index_groups=groups
        )

    def turn(values, by):
        pairs = [(g[i], g[(i + by) % side]) for g in rings for i in range(side)]
        return lax.ppermute(values, CYZ, pairs)

    core, y_at, z_at = (lax.axis_index(a) for a in CYZ)
    cols = jnp.stack([cols_in.reshape(-1), cols_out.reshape(-1)])
    cols = jnp.where(core == 0, cols, cols % nz * ny + cols // nz)
    place = jnp.where(core == 0, y_at, z_at)
    here = jnp.stack([core, place, lax.axis_index("x")]).astype(jnp.int32)
    here = jnp.pad(here, (0, rows * per_row - 3)).reshape(1, -1)
    opposite = (place + ny // 2) % ny
    lasts = jnp.where(cols // side == opposite, cols % side, side)
    where = jnp.concatenate([cols, here, lasts])

    mine = jnp.stack([inputs, upstream])
    unit = swap(jnp.broadcast_to(mine, (side, *mine.shape)), lines)
    dense = jax.ShapeDtypeStruct((side + 1, width, rows * width), BF16)
    in_last, out_last = pl.pallas_call(
        last_kernel,
        out_shape=(dense, dense),
        in_specs=[smem, vmem, vmem],
        out_specs=(vmem, vmem),
        compiler_params=params,
        name="last",
    )(where, w_in, w_out)
    unit, in_last, out_last = lax.optimization_barrier((unit, in_last, out_last))
    x_units, y_units = [unit[:, 0]], [unit[:, 1]]
    x_steps, y_steps = [0], [0]
    x_ahead = x_back = x_units[0]
    y_ahead = y_back = y_units[0]
    for s in range(1, side // 2):
        x_ahead, x_back = turn(x_ahead, 1), turn(x_back, -1)
        y_back, y_ahead = turn(y_back, -1), turn(y_ahead, 1)
        x_units += [x_ahead, x_back]
        y_units += [y_ahead, y_back]
        x_steps += [-s, s]
        y_steps += [-s, s]
    x_units.append(turn(x_ahead, 1))
    y_units.append(turn(y_back, -1))
    x_steps.append(-(side // 2))
    y_steps.append(side // 2)
    x_units, y_units = ([in_hbm(u) for u in us[:-1]] + us[-1:] for us in (x_units, y_units))
    x_plan, y_plan = (side, tuple(x_steps)), (side, tuple(y_steps))

    gathered = pltpu.VMEM((blocks, tok, width), BF16)
    loaded = pltpu.SemaphoreType.DMA((side,))
    values = pltpu.HBM((rows, tok, width), BF16)
    kept = pltpu.VMEM((tok, rows * width), F32)
    last = pltpu.VMEM((side, width, rows * width), BF16)
    hidden_most, grad_most, wi, li, lo = pl.pallas_call(
        functools.partial(early_kernel, ((side, x_plan[1][:-1]), (side, y_plan[1][:-1]))),
        out_shape=(kept, kept, pltpu.VMEM(w_in.shape, BF16), last, last),
        out_specs=(vmem,) * 5,
        in_specs=[smem] + [anywhere] * (len(x_units) + len(y_units) + 2),
        scratch_shapes=[
            pltpu.VMEM(w_out.shape, BF16),
            gathered,
            gathered,
            loaded,
            loaded,
            pltpu.SemaphoreType.DMA((4,)),
        ],
        compiler_params=params,
        name="early",
    )(where, *x_units[:-1], *y_units[:-1], *(in_hbm(v) for v in (w_in, w_out, in_last, out_last)))
    placed, act, grad = pl.pallas_call(
        back_kernel,
        out_shape=(pltpu.HBM((side, blocks // side, tok, width), BF16), values, values),
        in_specs=[smem] + [vmem] * 7,
        out_specs=(anywhere, anywhere, anywhere),
        scratch_shapes=[
            pltpu.VMEM((blocks, tok, width), F32),
            pltpu.VMEM((blocks, tok, width), BF16),
            pltpu.VMEM((rows, tok, width), BF16),
            pltpu.VMEM((rows, tok, width), BF16),
            pltpu.SemaphoreType.DMA((SLABS + 2,)),
        ],
        compiler_params=params,
        name="back",
    )(where, x_units[-1], y_units[-1], hidden_most, grad_most, wi, li, lo)

    on_ring = swap(placed, rings)

    half = jax.ShapeDtypeStruct((nx, 2, rows, each, width, width), BF16)
    own, other = pl.pallas_call(
        functools.partial(weight_kernel, (x_plan, y_plan)),
        out_shape=(half, half),
        in_specs=[smem] + [anywhere] * (len(x_units) + len(y_units) + 2),
        out_specs=(vmem, vmem),
        scratch_shapes=[
            gathered,
            gathered,
            pltpu.VMEM((rows, tok, width), BF16),
            pltpu.VMEM((rows, tok, width), BF16),
            loaded,
            loaded,
            pltpu.SemaphoreType.DMA((2,)),
        ],
        compiler_params=params,
        name="weights",
    )(where, *x_units, *y_units, act, grad)
    swapped = lax.ppermute(other, "c", [(0, 1), (1, 0)])
    paired = [(own[d].astype(F32) + swapped[d].astype(F32)).astype(BF16) for d in range(nx)]
    spread = [
        lax.ppermute(paired[d], "x", [(i, (i + d) % nx) for i in range(nx)]) for d in range(1, nx)
    ]
    summed = sum((v.astype(F32) for v in spread), paired[0].astype(F32)).astype(BF16)

    on_line = pl.pallas_call(
        sum_kernel,
        out_shape=jax.ShapeDtypeStruct(on_ring.shape[1:], BF16),
        in_specs=[vmem],
        out_specs=vmem,
        compiler_params=params,
        name="sums",
    )(pltpu.with_memory_space_constraint(on_ring, pltpu.VMEM))
    received = swap(on_line, lines)
    grad_inputs = jnp.sum(received.astype(F32), axis=0).astype(BF16)
    return grad_inputs, summed[0], summed[1]


def solution(mesh):
    n_dp, n_blk = mesh.devices.shape
    sizes = (n_dp // 2, 2, 8, n_blk // 8)
    fine = Mesh(mesh.devices.reshape(sizes), ("x", "c", "y", "z"))
    dp, blk = ("x", "c"), ("y", "z")
    return jax.shard_map(
        functools.partial(per_device, sizes),
        mesh=fine,
        in_specs=(
            P(dp, blk),
            P(dp, blk),
            P(blk, None, None, None),
            P(blk, None),
            P(blk, None, None, None),
            P(blk, None),
        ),
        out_specs=(P(dp, blk), P(blk, dp, None, None), P(blk, dp, None, None)),
        check_vma=False,
    )
```

```python
import functools

import jax
import jax.numpy as jnp
from jax import lax
from jax.experimental import pallas as pl
from jax.experimental.pallas import tpu as pltpu
from jax.sharding import Mesh, PartitionSpec as P

BF16 = jnp.bfloat16
F32 = jnp.float32
GELU_SCALE = 0.7978845608028654
GELU_CUBE = 0.044715
VMEM_LIMIT = 36 * 1024 * 1024
SLABS = 8
CYZ = ("c", "y", "z")


def dot_nn(a, b):
    return lax.dot_general(a, b, (((1,), (0,)), ((), ())), preferred_element_type=F32)


def dot_nt(a, b):
    return lax.dot_general(a, b, (((1,), (1,)), ((), ())), preferred_element_type=F32)


def dot_tn(a, b):
    return lax.dot_general(a, b, (((0,), (0,)), ((), ())), preferred_element_type=F32)


def repeat_kernel(first, second, out, both, sem, out_sem):
    loads = [
        pltpu.make_async_copy(ref, both.at[n], sem.at[n]) for n, ref in enumerate((first, second))
    ]
    stores = [pltpu.make_async_copy(both, out.at[s], out_sem.at[s]) for s in range(out.shape[0])]
    for copy in loads:
        copy.start()
    for copy in loads:
        copy.wait()
    for copy in stores:
        copy.start()
    for copy in stores:
        copy.wait()


def start_loads(where, units, into, sem, side):
    places = into.shape[0] // side
    loads = []
    for n, (ref, steps) in enumerate(units):
        place = lax.rem(where[2, 1] + (steps + places), places)
        loads.append(pltpu.make_async_copy(ref, into.at[pl.ds(place * side, side)], sem.at[n]))
        loads[-1].start()
    return loads


def row_of(blocks, where, line, r, per_row):
    return jnp.concatenate([blocks[where[line, r * per_row + k]] for k in range(per_row)], axis=1)


def last_kernel(where, w_in, w_out, in_last, out_last):
    rows, per_row, width, _ = w_in.shape
    in_last[...] = jnp.zeros_like(in_last)
    out_last[...] = jnp.zeros_like(out_last)
    for r in range(rows):
        at = slice(r * width, (r + 1) * width)
        for k in range(per_row):
            in_last[where[3, r * per_row + k], :, at] = w_in[r, k]
            out_last[where[4, r * per_row + k], :, at] = w_out[r, k].T


def early_kernel(plans, where, *refs):
    (side, x_steps), (_, y_steps) = plans
    n_x, n_y = len(x_steps), len(y_steps)
    x_units = list(zip(refs[:n_x], x_steps))
    y_units = list(zip(refs[n_x : n_x + n_y], y_steps))
    w_in, w_out, in_last, out_last = refs[n_x + n_y : n_x + n_y + 4]
    hidden, grad_act, wi, li, lo, wo, x, y, x_sem, y_sem, w_sem = refs[n_x + n_y + 4 :]
    rows, per_row, width, _ = w_in.shape
    load_in = pltpu.make_async_copy(w_in, wi, w_sem.at[0])
    load_out = pltpu.make_async_copy(w_out, wo, w_sem.at[1])
    load_in.start()
    x_loads = start_loads(where, x_units, x, x_sem, side)
    load_out.start()
    y_loads = start_loads(where, y_units, y, y_sem, side)
    lasts = [
        pltpu.make_async_copy(ref.at[pl.ds(0, side)], into, w_sem.at[2 + n])
        for n, (ref, into) in enumerate(((in_last, li), (out_last, lo)))
    ]
    for copy in lasts:
        copy.start()
    places = x.shape[0] // side
    opposite = pl.ds(lax.rem(where[2, 1] + places // 2, places) * side, side)
    x[opposite] = jnp.zeros((side, *x.shape[1:]), BF16)
    y[opposite] = jnp.zeros((side, *y.shape[1:]), BF16)
    load_in.wait()
    for copy in x_loads:
        copy.wait()
    for r in range(rows):
        x_row = row_of(x, where, 0, r, per_row)
        at = slice(r * width, (r + 1) * width)
        hidden[:, at] = dot_nn(x_row, wi[r].reshape(per_row * width, width))
    load_out.wait()
    for copy in y_loads:
        copy.wait()
    for r in range(rows):
        w_row = jnp.concatenate([wo[r, k] for k in range(per_row)], axis=1)
        at = slice(r * width, (r + 1) * width)
        grad_act[:, at] = dot_nt(row_of(y, where, 1, r, per_row), w_row)
    for copy in lasts:
        copy.wait()


def back_kernel(where, x_last, y_last, hidden_most, grad_most, wi, li, lo, *refs):
    placed, act_out, grad_out, total, rounded, act, grad, out_sem = refs
    rows, per_row, width, _ = wi.shape
    blocks, side = total.shape[0], x_last.shape[0]
    total[...] = jnp.zeros_like(total)
    x_unit = jnp.concatenate([x_last[n] for n in range(side)], axis=1)
    y_unit = jnp.concatenate([y_last[n] for n in range(side)], axis=1)
    hidden = hidden_most[...] + dot_nn(x_unit, li[...].reshape(side * width, rows * width))
    grad_act = grad_most[...] + dot_nn(y_unit, lo[...].reshape(side * width, rows * width))
    square = hidden * hidden
    tanh = jnp.tanh(GELU_SCALE * hidden * (1.0 + GELU_CUBE * square))
    half = 0.5 * (1.0 + tanh)
    slope = half + 0.5 * hidden * (1.0 - tanh * tanh) * (
        GELU_SCALE * (1.0 + 3.0 * GELU_CUBE * square)
    )
    activated = (hidden * half).astype(BF16)
    grad_hidden = (grad_act * slope).astype(BF16)
    for r in range(rows):
        at = slice(r * width, (r + 1) * width)
        act[r] = activated[:, at]
        grad[r] = grad_hidden[:, at]
    stores = [
        pltpu.make_async_copy(act, act_out, out_sem.at[SLABS]),
        pltpu.make_async_copy(grad, grad_out, out_sem.at[SLABS + 1]),
    ]
    for copy in stores:
        copy.start()
    for r in range(rows):
        at = slice(r * width, (r + 1) * width)
        terms = dot_nt(grad_hidden[:, at], wi[r].reshape(per_row * width, width))
        for k in range(per_row):
            c = where[0, r * per_row + k]
            total[c] = total[c] + terms[:, k * width : (k + 1) * width]
    slab = blocks // SLABS
    for s in range(SLABS):
        at = pl.ds(s * slab, slab)
        rounded[at] = total[at].astype(BF16)
        stores.append(pltpu.make_async_copy(rounded.at[at], placed.at[s], out_sem.at[s]))
        stores[-1].start()
    for copy in stores:
        copy.wait()


def weight_kernel(plans, where, *refs):
    (side, x_steps), (_, y_steps) = plans
    n_x, n_y = len(x_steps), len(y_steps)
    act_in, grad_in, own, other, x, y, act, grad, x_sem, y_sem, sem = refs[n_x + n_y :]
    loads = [
        pltpu.make_async_copy(act_in, act, sem.at[0]),
        pltpu.make_async_copy(grad_in, grad, sem.at[1]),
    ]
    for copy in loads:
        copy.start()
    loads += start_loads(where, list(zip(refs[:n_x], x_steps)), x, x_sem, side)
    loads += start_loads(where, list(zip(refs[n_x : n_x + n_y], y_steps)), y, y_sem, side)
    for copy in loads:
        copy.wait()
    xs, _, rows, each, width, _ = own.shape
    per_row = xs * 2 * each
    core = where[2, 0]
    for r in range(rows):
        act_t = act[r].T
        grad_r = grad[r]
        for away in range(xs):
            x_at = lax.rem(where[2, 2] + away, xs)
            for half, out in ((core, own), (1 - core, other)):
                for j in range(each):
                    at = r * per_row + (x_at * 2 + half) * each + j
                    out[away, 0, r, j] = dot_tn(x[where[0, at]], grad_r).astype(BF16)
                    out[away, 1, r, j] = dot_nn(act_t, y[where[1, at]]).astype(BF16)


def sum_kernel(parts, out):
    for n in range(parts.shape[1]):
        kept = parts[0, n].astype(F32)
        for s in range(1, parts.shape[0]):
            kept = kept + parts[s, n].astype(F32)
        out[n] = kept.astype(BF16)


def lines_and_rings(ny, nz):
    along_z = [[y * nz + z for z in range(nz)] for y in range(ny)]
    along_y = [[y * nz + z for y in range(ny)] for z in range(nz)]
    second = [[[ny * nz + p for p in group] for group in groups] for groups in (along_z, along_y)]
    return along_z + second[1], along_y + second[0]


def per_device(sizes, inputs, upstream, w_in, cols_in, w_out, cols_out):
    nx, nc, ny, nz = sizes
    side = nz
    tok, width = inputs.shape
    rows, per_row = cols_in.shape
    each = per_row // (nx * nc)
    blocks = ny * nz
    lines, rings = lines_and_rings(ny, nz)
    smem = pl.BlockSpec(memory_space=pltpu.SMEM)
    vmem = pl.BlockSpec(memory_space=pltpu.VMEM)
    anywhere = pl.BlockSpec(memory_space=pl.ANY)
    params = pltpu.CompilerParams(vmem_limit_bytes=VMEM_LIMIT)

    def in_hbm(values):
        return pltpu.with_memory_space_constraint(values, pltpu.HBM)

    def swap(values, groups):
        return lax.all_to_all(
            values, CYZ, split_axis=0, concat_axis=0, tiled=True, axis_index_groups=groups
        )

    def turn(values, by):
        pairs = [(g[i], g[(i + by) % side]) for g in rings for i in range(side)]
        return lax.ppermute(values, CYZ, pairs)

    core, y_at, z_at = (lax.axis_index(a) for a in CYZ)
    cols = jnp.stack([cols_in.reshape(-1), cols_out.reshape(-1)])
    cols = jnp.where(core == 0, cols, cols % nz * ny + cols // nz)
    place = jnp.where(core == 0, y_at, z_at)
    here = jnp.stack([core, place, lax.axis_index("x")]).astype(jnp.int32)
    here = jnp.pad(here, (0, rows * per_row - 3)).reshape(1, -1)
    opposite = (place + ny // 2) % ny
    lasts = jnp.where(cols // side == opposite, cols % side, side)
    where = jnp.concatenate([cols, here, lasts])

    mine = pl.pallas_call(
        repeat_kernel,
        out_shape=jax.ShapeDtypeStruct((side, 2, tok, width), BF16),
        in_specs=[anywhere, anywhere],
        out_specs=anywhere,
        scratch_shapes=[
            pltpu.VMEM((2, tok, width), BF16),
            pltpu.SemaphoreType.DMA((2,)),
            pltpu.SemaphoreType.DMA((side,)),
        ],
        compiler_params=params,
        name="repeat",
    )(in_hbm(inputs), in_hbm(upstream))
    unit = swap(mine, lines)
    dense = jax.ShapeDtypeStruct((side + 1, width, rows * width), BF16)
    in_last, out_last = pl.pallas_call(
        last_kernel,
        out_shape=(dense, dense),
        in_specs=[smem, vmem, vmem],
        out_specs=(vmem, vmem),
        compiler_params=params,
        name="last",
    )(where, w_in, w_out)
    unit, in_last, out_last = lax.optimization_barrier((unit, in_last, out_last))
    x_units, y_units = [unit[:, 0]], [unit[:, 1]]
    x_steps, y_steps = [0], [0]
    x_ahead = x_back = x_units[0]
    y_ahead = y_back = y_units[0]
    for s in range(1, side // 2):
        x_ahead, x_back = turn(x_ahead, 1), turn(x_back, -1)
        y_back, y_ahead = turn(y_back, -1), turn(y_ahead, 1)
        x_units += [x_ahead, x_back]
        y_units += [y_ahead, y_back]
        x_steps += [-s, s]
        y_steps += [-s, s]
    x_units.append(turn(x_ahead, 1))
    y_units.append(turn(y_back, -1))
    x_steps.append(-(side // 2))
    y_steps.append(side // 2)
    x_units, y_units = ([in_hbm(u) for u in us[:-3]] + us[-3:] for us in (x_units, y_units))
    x_plan, y_plan = (side, tuple(x_steps)), (side, tuple(y_steps))

    gathered = pltpu.VMEM((blocks, tok, width), BF16)
    loaded = pltpu.SemaphoreType.DMA((side,))
    values = pltpu.HBM((rows, tok, width), BF16)
    kept = pltpu.VMEM((tok, rows * width), F32)
    last = pltpu.VMEM((side, width, rows * width), BF16)
    hidden_most, grad_most, wi, li, lo = pl.pallas_call(
        functools.partial(early_kernel, ((side, x_plan[1][:-1]), (side, y_plan[1][:-1]))),
        out_shape=(kept, kept, pltpu.VMEM(w_in.shape, BF16), last, last),
        out_specs=(vmem,) * 5,
        in_specs=[smem] + [anywhere] * (len(x_units) + len(y_units) + 2),
        scratch_shapes=[
            pltpu.VMEM(w_out.shape, BF16),
            gathered,
            gathered,
            loaded,
            loaded,
            pltpu.SemaphoreType.DMA((4,)),
        ],
        compiler_params=params,
        name="early",
    )(where, *x_units[:-1], *y_units[:-1], *(in_hbm(v) for v in (w_in, w_out, in_last, out_last)))
    placed, act, grad = pl.pallas_call(
        back_kernel,
        out_shape=(pltpu.HBM((side, blocks // side, tok, width), BF16), values, values),
        in_specs=[smem] + [vmem] * 7,
        out_specs=(anywhere, anywhere, anywhere),
        scratch_shapes=[
            pltpu.VMEM((blocks, tok, width), F32),
            pltpu.VMEM((blocks, tok, width), BF16),
            pltpu.VMEM((rows, tok, width), BF16),
            pltpu.VMEM((rows, tok, width), BF16),
            pltpu.SemaphoreType.DMA((SLABS + 2,)),
        ],
        compiler_params=params,
        name="back",
    )(where, x_units[-1], y_units[-1], hidden_most, grad_most, wi, li, lo)

    on_ring = swap(placed, rings)

    half = jax.ShapeDtypeStruct((nx, 2, rows, each, width, width), BF16)
    own, other = pl.pallas_call(
        functools.partial(weight_kernel, (x_plan, y_plan)),
        out_shape=(half, half),
        in_specs=[smem] + [anywhere] * (len(x_units) + len(y_units) + 2),
        out_specs=(vmem, vmem),
        scratch_shapes=[
            gathered,
            gathered,
            pltpu.VMEM((rows, tok, width), BF16),
            pltpu.VMEM((rows, tok, width), BF16),
            loaded,
            loaded,
            pltpu.SemaphoreType.DMA((2,)),
        ],
        compiler_params=params,
        name="weights",
    )(where, *x_units, *y_units, act, grad)
    swapped = lax.ppermute(other, "c", [(0, 1), (1, 0)])
    paired = [(own[d].astype(F32) + swapped[d].astype(F32)).astype(BF16) for d in range(nx)]
    spread = [
        lax.ppermute(paired[d], "x", [(i, (i + d) % nx) for i in range(nx)]) for d in range(1, nx)
    ]
    summed = sum((v.astype(F32) for v in spread), paired[0].astype(F32)).astype(BF16)

    on_line = pl.pallas_call(
        sum_kernel,
        out_shape=jax.ShapeDtypeStruct(on_ring.shape[1:], BF16),
        in_specs=[vmem],
        out_specs=vmem,
        compiler_params=params,
        name="sums",
    )(pltpu.with_memory_space_constraint(on_ring, pltpu.VMEM))
    received = swap(on_line, lines)
    grad_inputs = jnp.sum(received.astype(F32), axis=0).astype(BF16)
    return grad_inputs, summed[0], summed[1]


def solution(mesh):
    n_dp, n_blk = mesh.devices.shape
    sizes = (n_dp // 2, 2, 8, n_blk // 8)
    fine = Mesh(mesh.devices.reshape(sizes), ("x", "c", "y", "z"))
    dp, blk = ("x", "c"), ("y", "z")
    return jax.shard_map(
        functools.partial(per_device, sizes),
        mesh=fine,
        in_specs=(
            P(dp, blk),
            P(dp, blk),
            P(blk, None, None, None),
            P(blk, None),
            P(blk, None, None, None),
            P(blk, None),
        ),
        out_specs=(P(dp, blk), P(blk, dp, None, None), P(blk, dp, None, None)),
        check_vma=False,
    )
```

```python
import functools

import jax
import jax.numpy as jnp
from jax import lax
from jax.experimental import pallas as pl
from jax.experimental.pallas import tpu as pltpu
from jax.sharding import Mesh, PartitionSpec as P

BF16 = jnp.bfloat16
F32 = jnp.float32
GELU_SCALE = 0.7978845608028654
GELU_CUBE = 0.044715
VMEM_LIMIT = 36 * 1024 * 1024
SLABS = 8
CYZ = ("c", "y", "z")


def dot_nn(a, b):
    return lax.dot_general(a, b, (((1,), (0,)), ((), ())), preferred_element_type=F32)


def dot_nt(a, b):
    return lax.dot_general(a, b, (((1,), (1,)), ((), ())), preferred_element_type=F32)


def dot_tn(a, b):
    return lax.dot_general(a, b, (((0,), (0,)), ((), ())), preferred_element_type=F32)


def start_loads(where, units, into, sem, side):
    places = into.shape[0] // side
    loads = []
    for n, (ref, steps) in enumerate(units):
        place = lax.rem(where[2, 1] + (steps + places), places)
        loads.append(pltpu.make_async_copy(ref, into.at[pl.ds(place * side, side)], sem.at[n]))
        loads[-1].start()
    return loads


def row_of(blocks, where, line, r, per_row):
    return jnp.concatenate([blocks[where[line, r * per_row + k]] for k in range(per_row)], axis=1)


def early_kernel(plans, where, *refs):
    (side, x_steps), (_, y_steps) = plans
    n_x, n_y = len(x_steps), len(y_steps)
    x_units = list(zip(refs[:n_x], x_steps))
    y_units = list(zip(refs[n_x : n_x + n_y], y_steps))
    w_in, w_out = refs[n_x + n_y : n_x + n_y + 2]
    hidden, grad_act, wi, in_last, out_last, wo, x, y, x_sem, y_sem, w_sem = refs[n_x + n_y + 2 :]
    rows, per_row, width, _ = w_in.shape
    load_in = pltpu.make_async_copy(w_in, wi, w_sem.at[0])
    load_out = pltpu.make_async_copy(w_out, wo, w_sem.at[1])
    load_in.start()
    load_out.start()
    x_loads = start_loads(where, x_units, x, x_sem, side)
    y_loads = start_loads(where, y_units, y, y_sem, side)
    in_last[...] = jnp.zeros_like(in_last)
    out_last[...] = jnp.zeros_like(out_last)
    places = x.shape[0] // side
    opposite = pl.ds(lax.rem(where[2, 1] + places // 2, places) * side, side)
    x[opposite] = jnp.zeros((side, *x.shape[1:]), BF16)
    y[opposite] = jnp.zeros((side, *y.shape[1:]), BF16)
    load_in.wait()
    load_out.wait()
    for r in range(rows):
        at = slice(r * width, (r + 1) * width)
        for k in range(per_row):
            in_last[where[3, r * per_row + k], :, at] = wi[r, k]
            out_last[where[4, r * per_row + k], :, at] = wo[r, k].T
    for copy in x_loads:
        copy.wait()
    for r in range(rows):
        x_row = row_of(x, where, 0, r, per_row)
        at = slice(r * width, (r + 1) * width)
        hidden[:, at] = dot_nn(x_row, wi[r].reshape(per_row * width, width))
    for copy in y_loads:
        copy.wait()
    for r in range(rows):
        w_row = jnp.concatenate([wo[r, k] for k in range(per_row)], axis=1)
        at = slice(r * width, (r + 1) * width)
        grad_act[:, at] = dot_nt(row_of(y, where, 1, r, per_row), w_row)


def back_kernel(where, x_last, y_last, hidden_most, grad_most, wi, li, lo, *refs):
    placed, act_out, grad_out, total, rounded, act, grad, out_sem = refs
    rows, per_row, width, _ = wi.shape
    blocks, side = total.shape[0], x_last.shape[0]
    total[...] = jnp.zeros_like(total)
    x_unit = jnp.concatenate([x_last[n] for n in range(side)], axis=1)
    y_unit = jnp.concatenate([y_last[n] for n in range(side)], axis=1)
    hidden = hidden_most[...] + dot_nn(x_unit, li[:side].reshape(side * width, rows * width))
    grad_act = grad_most[...] + dot_nn(y_unit, lo[:side].reshape(side * width, rows * width))
    square = hidden * hidden
    tanh = jnp.tanh(GELU_SCALE * hidden * (1.0 + GELU_CUBE * square))
    half = 0.5 * (1.0 + tanh)
    slope = half + 0.5 * hidden * (1.0 - tanh * tanh) * (
        GELU_SCALE * (1.0 + 3.0 * GELU_CUBE * square)
    )
    activated = (hidden * half).astype(BF16)
    grad_hidden = (grad_act * slope).astype(BF16)
    for r in range(rows):
        at = slice(r * width, (r + 1) * width)
        act[r] = activated[:, at]
        grad[r] = grad_hidden[:, at]
    stores = [
        pltpu.make_async_copy(act, act_out, out_sem.at[SLABS]),
        pltpu.make_async_copy(grad, grad_out, out_sem.at[SLABS + 1]),
    ]
    for copy in stores:
        copy.start()
    for r in range(rows):
        at = slice(r * width, (r + 1) * width)
        terms = dot_nt(grad_hidden[:, at], wi[r].reshape(per_row * width, width))
        for k in range(per_row):
            c = where[0, r * per_row + k]
            total[c] = total[c] + terms[:, k * width : (k + 1) * width]
    slab = blocks // SLABS
    for s in range(SLABS):
        at = pl.ds(s * slab, slab)
        rounded[at] = total[at].astype(BF16)
        stores.append(pltpu.make_async_copy(rounded.at[at], placed.at[s], out_sem.at[s]))
        stores[-1].start()
    for copy in stores:
        copy.wait()


def weight_kernel(plans, where, *refs):
    (side, x_steps), (_, y_steps) = plans
    n_x, n_y = len(x_steps), len(y_steps)
    act_in, grad_in, own, other, x, y, act, grad, x_sem, y_sem, sem = refs[n_x + n_y :]
    loads = [
        pltpu.make_async_copy(act_in, act, sem.at[0]),
        pltpu.make_async_copy(grad_in, grad, sem.at[1]),
    ]
    for copy in loads:
        copy.start()
    loads += start_loads(where, list(zip(refs[:n_x], x_steps)), x, x_sem, side)
    loads += start_loads(where, list(zip(refs[n_x : n_x + n_y], y_steps)), y, y_sem, side)
    for copy in loads:
        copy.wait()
    xs, _, rows, each, width, _ = own.shape
    per_row = xs * 2 * each
    core = where[2, 0]
    for r in range(rows):
        act_t = act[r].T
        grad_r = grad[r]
        for away in range(xs):
            x_at = lax.rem(where[2, 2] + away, xs)
            for half, out in ((core, own), (1 - core, other)):
                for j in range(each):
                    at = r * per_row + (x_at * 2 + half) * each + j
                    out[away, 0, r, j] = dot_tn(x[where[0, at]], grad_r).astype(BF16)
                    out[away, 1, r, j] = dot_nn(act_t, y[where[1, at]]).astype(BF16)


def sum_kernel(parts, out):
    for n in range(parts.shape[1]):
        kept = parts[0, n].astype(F32)
        for s in range(1, parts.shape[0]):
            kept = kept + parts[s, n].astype(F32)
        out[n] = kept.astype(BF16)


def lines_and_rings(ny, nz):
    along_z = [[y * nz + z for z in range(nz)] for y in range(ny)]
    along_y = [[y * nz + z for y in range(ny)] for z in range(nz)]
    second = [[[ny * nz + p for p in group] for group in groups] for groups in (along_z, along_y)]
    return along_z + second[1], along_y + second[0]


def per_device(sizes, inputs, upstream, w_in, cols_in, w_out, cols_out):
    nx, nc, ny, nz = sizes
    side = nz
    tok, width = inputs.shape
    rows, per_row = cols_in.shape
    each = per_row // (nx * nc)
    blocks = ny * nz
    lines, rings = lines_and_rings(ny, nz)
    smem = pl.BlockSpec(memory_space=pltpu.SMEM)
    vmem = pl.BlockSpec(memory_space=pltpu.VMEM)
    anywhere = pl.BlockSpec(memory_space=pl.ANY)
    params = pltpu.CompilerParams(vmem_limit_bytes=VMEM_LIMIT)

    def in_hbm(values):
        return pltpu.with_memory_space_constraint(values, pltpu.HBM)

    def swap(values, groups):
        return lax.all_to_all(
            values, CYZ, split_axis=0, concat_axis=0, tiled=True, axis_index_groups=groups
        )

    def turn(values, by):
        pairs = [(g[i], g[(i + by) % side]) for g in rings for i in range(side)]
        return lax.ppermute(values, CYZ, pairs)

    core, y_at, z_at = (lax.axis_index(a) for a in CYZ)
    cols = jnp.stack([cols_in.reshape(-1), cols_out.reshape(-1)])
    cols = jnp.where(core == 0, cols, cols % nz * ny + cols // nz)
    place = jnp.where(core == 0, y_at, z_at)
    here = jnp.stack([core, place, lax.axis_index("x")]).astype(jnp.int32)
    here = jnp.pad(here, (0, rows * per_row - 3)).reshape(1, -1)
    opposite = (place + ny // 2) % ny
    lasts = jnp.where(cols // side == opposite, cols % side, side)
    where = jnp.concatenate([cols, here, lasts])

    mine = jnp.stack([inputs, upstream])
    unit = swap(jnp.broadcast_to(mine, (side, *mine.shape)), lines)
    x_units, y_units = [unit[:, 0]], [unit[:, 1]]
    x_steps, y_steps = [0], [0]
    x_ahead = x_back = x_units[0]
    y_ahead = y_back = y_units[0]
    for s in range(1, side // 2):
        x_ahead, x_back = turn(x_ahead, 1), turn(x_back, -1)
        y_back, y_ahead = turn(y_back, -1), turn(y_ahead, 1)
        x_units += [x_ahead, x_back]
        y_units += [y_ahead, y_back]
        x_steps += [-s, s]
        y_steps += [-s, s]
    x_units.append(turn(x_ahead, 1))
    y_units.append(turn(y_back, -1))
    x_steps.append(-(side // 2))
    y_steps.append(side // 2)
    x_units, y_units = ([in_hbm(u) for u in us[:-3]] + us[-3:] for us in (x_units, y_units))
    x_plan, y_plan = (side, tuple(x_steps)), (side, tuple(y_steps))

    gathered = pltpu.VMEM((blocks, tok, width), BF16)
    loaded = pltpu.SemaphoreType.DMA((side,))
    values = pltpu.HBM((rows, tok, width), BF16)
    kept = pltpu.VMEM((tok, rows * width), F32)
    last = pltpu.VMEM((side + 1, width, rows * width), BF16)
    hidden_most, grad_most, wi, li, lo = pl.pallas_call(
        functools.partial(early_kernel, ((side, x_plan[1][:-1]), (side, y_plan[1][:-1]))),
        out_shape=(kept, kept, pltpu.VMEM(w_in.shape, BF16), last, last),
        out_specs=(vmem,) * 5,
        in_specs=[smem] + [anywhere] * (len(x_units) + len(y_units)),
        scratch_shapes=[
            pltpu.VMEM(w_out.shape, BF16),
            gathered,
            gathered,
            loaded,
            loaded,
            pltpu.SemaphoreType.DMA((2,)),
        ],
        compiler_params=params,
        name="early",
    )(where, *x_units[:-1], *y_units[:-1], in_hbm(w_in), in_hbm(w_out))
    placed, act, grad = pl.pallas_call(
        back_kernel,
        out_shape=(pltpu.HBM((side, blocks // side, tok, width), BF16), values, values),
        in_specs=[smem] + [vmem] * 7,
        out_specs=(anywhere, anywhere, anywhere),
        scratch_shapes=[
            pltpu.VMEM((blocks, tok, width), F32),
            pltpu.VMEM((blocks, tok, width), BF16),
            pltpu.VMEM((rows, tok, width), BF16),
            pltpu.VMEM((rows, tok, width), BF16),
            pltpu.SemaphoreType.DMA((SLABS + 2,)),
        ],
        compiler_params=params,
        name="back",
    )(where, x_units[-1], y_units[-1], hidden_most, grad_most, wi, li, lo)

    on_ring = swap(placed, rings)

    half = jax.ShapeDtypeStruct((nx, 2, rows, each, width, width), BF16)
    own, other = pl.pallas_call(
        functools.partial(weight_kernel, (x_plan, y_plan)),
        out_shape=(half, half),
        in_specs=[smem] + [anywhere] * (len(x_units) + len(y_units) + 2),
        out_specs=(vmem, vmem),
        scratch_shapes=[
            gathered,
            gathered,
            pltpu.VMEM((rows, tok, width), BF16),
            pltpu.VMEM((rows, tok, width), BF16),
            loaded,
            loaded,
            pltpu.SemaphoreType.DMA((2,)),
        ],
        compiler_params=params,
        name="weights",
    )(where, *(in_hbm(v) for v in (*x_units, *y_units)), act, grad)
    swapped = lax.ppermute(other, "c", [(0, 1), (1, 0)])
    paired = [(own[d].astype(F32) + swapped[d].astype(F32)).astype(BF16) for d in range(nx)]
    spread = [
        lax.ppermute(paired[d], "x", [(i, (i + d) % nx) for i in range(nx)]) for d in range(1, nx)
    ]
    summed = sum((v.astype(F32) for v in spread), paired[0].astype(F32)).astype(BF16)

    on_line = pl.pallas_call(
        sum_kernel,
        out_shape=jax.ShapeDtypeStruct(on_ring.shape[1:], BF16),
        in_specs=[vmem],
        out_specs=vmem,
        compiler_params=params,
        name="sums",
    )(pltpu.with_memory_space_constraint(on_ring, pltpu.VMEM))
    received = swap(on_line, lines)
    grad_inputs = jnp.sum(received.astype(F32), axis=0).astype(BF16)
    return grad_inputs, summed[0], summed[1]


def solution(mesh):
    n_dp, n_blk = mesh.devices.shape
    sizes = (n_dp // 2, 2, 8, n_blk // 8)
    fine = Mesh(mesh.devices.reshape(sizes), ("x", "c", "y", "z"))
    dp, blk = ("x", "c"), ("y", "z")
    return jax.shard_map(
        functools.partial(per_device, sizes),
        mesh=fine,
        in_specs=(
            P(dp, blk),
            P(dp, blk),
            P(blk, None, None, None),
            P(blk, None),
            P(blk, None, None, None),
            P(blk, None),
        ),
        out_specs=(P(dp, blk), P(blk, dp, None, None), P(blk, dp, None, None)),
        check_vma=False,
    )
```

```python
import functools

import jax
import jax.numpy as jnp
from jax import lax
from jax.experimental import pallas as pl
from jax.experimental.pallas import tpu as pltpu
from jax.sharding import Mesh, PartitionSpec as P

BF16 = jnp.bfloat16
F32 = jnp.float32
GELU_SCALE = 0.7978845608028654
GELU_CUBE = 0.044715
VMEM_LIMIT = 36 * 1024 * 1024
SLABS = 8
CYZ = ("c", "y", "z")


def dot_nn(a, b):
    return lax.dot_general(a, b, (((1,), (0,)), ((), ())), preferred_element_type=F32)


def dot_nt(a, b):
    return lax.dot_general(a, b, (((1,), (1,)), ((), ())), preferred_element_type=F32)


def dot_tn(a, b):
    return lax.dot_general(a, b, (((0,), (0,)), ((), ())), preferred_element_type=F32)


def start_loads(where, units, into, sem, side):
    places = into.shape[0] // side
    loads = []
    for n, (ref, steps) in enumerate(units):
        place = lax.rem(where[2, 1] + (steps + places), places)
        loads.append(pltpu.make_async_copy(ref, into.at[pl.ds(place * side, side)], sem.at[n]))
        loads[-1].start()
    return loads


def row_of(blocks, where, line, r, per_row):
    return jnp.concatenate([blocks[where[line, r * per_row + k]] for k in range(per_row)], axis=1)


def early_kernel(plans, where, *refs):
    (side, x_steps), (_, y_steps) = plans
    n_x, n_y = len(x_steps), len(y_steps)
    x_units = list(zip(refs[:n_x], x_steps))
    y_units = list(zip(refs[n_x : n_x + n_y], y_steps))
    w_in, w_out = refs[n_x + n_y : n_x + n_y + 2]
    hidden, grad_act, wi, in_last, out_last, total, wo, x, y, x_sem, y_sem, w_sem = refs[n_x + n_y + 2 :]
    rows, per_row, width, _ = w_in.shape
    load_in = pltpu.make_async_copy(w_in, wi, w_sem.at[0])
    load_out = pltpu.make_async_copy(w_out, wo, w_sem.at[1])
    load_in.start()
    load_out.start()
    x_loads = start_loads(where, x_units, x, x_sem, side)
    y_loads = start_loads(where, y_units, y, y_sem, side)
    total[...] = jnp.zeros_like(total)
    in_last[...] = jnp.zeros_like(in_last)
    out_last[...] = jnp.zeros_like(out_last)
    places = x.shape[0] // side
    opposite = pl.ds(lax.rem(where[2, 1] + places // 2, places) * side, side)
    x[opposite] = jnp.zeros((side, *x.shape[1:]), BF16)
    y[opposite] = jnp.zeros((side, *y.shape[1:]), BF16)
    load_in.wait()
    load_out.wait()
    for r in range(rows):
        at = slice(r * width, (r + 1) * width)
        for k in range(per_row):
            in_last[where[3, r * per_row + k], :, at] = wi[r, k]
            out_last[where[4, r * per_row + k], :, at] = wo[r, k].T
    for copy in x_loads:
        copy.wait()
    for r in range(rows):
        x_row = row_of(x, where, 0, r, per_row)
        at = slice(r * width, (r + 1) * width)
        hidden[:, at] = dot_nn(x_row, wi[r].reshape(per_row * width, width))
    for copy in y_loads:
        copy.wait()
    for r in range(rows):
        w_row = jnp.concatenate([wo[r, k] for k in range(per_row)], axis=1)
        at = slice(r * width, (r + 1) * width)
        grad_act[:, at] = dot_nt(row_of(y, where, 1, r, per_row), w_row)


def back_kernel(where, x_last, y_last, hidden_most, grad_most, wi, li, lo, zeros, *refs):
    placed, act_out, grad_out, total, rounded, act, grad, out_sem = refs
    rows, per_row, width, _ = wi.shape
    blocks, side = total.shape[0], x_last.shape[0]
    x_unit = jnp.concatenate([x_last[n] for n in range(side)], axis=1)
    y_unit = jnp.concatenate([y_last[n] for n in range(side)], axis=1)
    hidden = hidden_most[...] + dot_nn(x_unit, li[:side].reshape(side * width, rows * width))
    grad_act = grad_most[...] + dot_nn(y_unit, lo[:side].reshape(side * width, rows * width))
    square = hidden * hidden
    tanh = jnp.tanh(GELU_SCALE * hidden * (1.0 + GELU_CUBE * square))
    half = 0.5 * (1.0 + tanh)
    slope = half + 0.5 * hidden * (1.0 - tanh * tanh) * (
        GELU_SCALE * (1.0 + 3.0 * GELU_CUBE * square)
    )
    activated = (hidden * half).astype(BF16)
    grad_hidden = (grad_act * slope).astype(BF16)
    for r in range(rows):
        at = slice(r * width, (r + 1) * width)
        act[r] = activated[:, at]
        grad[r] = grad_hidden[:, at]
    stores = [
        pltpu.make_async_copy(act, act_out, out_sem.at[SLABS]),
        pltpu.make_async_copy(grad, grad_out, out_sem.at[SLABS + 1]),
    ]
    for copy in stores:
        copy.start()
    for r in range(rows):
        at = slice(r * width, (r + 1) * width)
        terms = dot_nt(grad_hidden[:, at], wi[r].reshape(per_row * width, width))
        for k in range(per_row):
            c = where[0, r * per_row + k]
            total[c] = total[c] + terms[:, k * width : (k + 1) * width]
    slab = blocks // SLABS
    for s in range(SLABS):
        at = pl.ds(s * slab, slab)
        rounded[at] = total[at].astype(BF16)
        stores.append(pltpu.make_async_copy(rounded.at[at], placed.at[s], out_sem.at[s]))
        stores[-1].start()
    for copy in stores:
        copy.wait()


def weight_kernel(plans, where, *refs):
    (side, x_steps), (_, y_steps) = plans
    n_x, n_y = len(x_steps), len(y_steps)
    act_in, grad_in, own, other, x, y, act, grad, x_sem, y_sem, sem = refs[n_x + n_y :]
    loads = [
        pltpu.make_async_copy(act_in, act, sem.at[0]),
        pltpu.make_async_copy(grad_in, grad, sem.at[1]),
    ]
    for copy in loads:
        copy.start()
    loads += start_loads(where, list(zip(refs[:n_x], x_steps)), x, x_sem, side)
    loads += start_loads(where, list(zip(refs[n_x : n_x + n_y], y_steps)), y, y_sem, side)
    for copy in loads:
        copy.wait()
    xs, _, rows, each, width, _ = own.shape
    per_row = xs * 2 * each
    core = where[2, 0]
    for r in range(rows):
        act_t = act[r].T
        grad_r = grad[r]
        for away in range(xs):
            x_at = lax.rem(where[2, 2] + away, xs)
            for half, out in ((core, own), (1 - core, other)):
                for j in range(each):
                    at = r * per_row + (x_at * 2 + half) * each + j
                    out[away, 0, r, j] = dot_tn(x[where[0, at]], grad_r).astype(BF16)
                    out[away, 1, r, j] = dot_nn(act_t, y[where[1, at]]).astype(BF16)


def sum_kernel(parts, out):
    for n in range(parts.shape[1]):
        kept = parts[0, n].astype(F32)
        for s in range(1, parts.shape[0]):
            kept = kept + parts[s, n].astype(F32)
        out[n] = kept.astype(BF16)


def lines_and_rings(ny, nz):
    along_z = [[y * nz + z for z in range(nz)] for y in range(ny)]
    along_y = [[y * nz + z for y in range(ny)] for z in range(nz)]
    second = [[[ny * nz + p for p in group] for group in groups] for groups in (along_z, along_y)]
    return along_z + second[1], along_y + second[0]


def per_device(sizes, inputs, upstream, w_in, cols_in, w_out, cols_out):
    nx, nc, ny, nz = sizes
    side = nz
    tok, width = inputs.shape
    rows, per_row = cols_in.shape
    each = per_row // (nx * nc)
    blocks = ny * nz
    lines, rings = lines_and_rings(ny, nz)
    smem = pl.BlockSpec(memory_space=pltpu.SMEM)
    vmem = pl.BlockSpec(memory_space=pltpu.VMEM)
    anywhere = pl.BlockSpec(memory_space=pl.ANY)
    params = pltpu.CompilerParams(vmem_limit_bytes=VMEM_LIMIT)

    def in_hbm(values):
        return pltpu.with_memory_space_constraint(values, pltpu.HBM)

    def swap(values, groups):
        return lax.all_to_all(
            values, CYZ, split_axis=0, concat_axis=0, tiled=True, axis_index_groups=groups
        )

    def turn(values, by):
        pairs = [(g[i], g[(i + by) % side]) for g in rings for i in range(side)]
        return lax.ppermute(values, CYZ, pairs)

    core, y_at, z_at = (lax.axis_index(a) for a in CYZ)
    cols = jnp.stack([cols_in.reshape(-1), cols_out.reshape(-1)])
    cols = jnp.where(core == 0, cols, cols % nz * ny + cols // nz)
    place = jnp.where(core == 0, y_at, z_at)
    here = jnp.stack([core, place, lax.axis_index("x")]).astype(jnp.int32)
    here = jnp.pad(here, (0, rows * per_row - 3)).reshape(1, -1)
    opposite = (place + ny // 2) % ny
    lasts = jnp.where(cols // side == opposite, cols % side, side)
    where = jnp.concatenate([cols, here, lasts])

    mine = jnp.stack([inputs, upstream])
    unit = swap(jnp.broadcast_to(mine, (side, *mine.shape)), lines)
    x_units, y_units = [unit[:, 0]], [unit[:, 1]]
    x_steps, y_steps = [0], [0]
    x_ahead = x_back = x_units[0]
    y_ahead = y_back = y_units[0]
    for s in range(1, side // 2):
        x_ahead, x_back = turn(x_ahead, 1), turn(x_back, -1)
        y_back, y_ahead = turn(y_back, -1), turn(y_ahead, 1)
        x_units += [x_ahead, x_back]
        y_units += [y_ahead, y_back]
        x_steps += [-s, s]
        y_steps += [-s, s]
    x_units.append(turn(x_ahead, 1))
    y_units.append(turn(y_back, -1))
    x_steps.append(-(side // 2))
    y_steps.append(side // 2)
    x_units, y_units = ([in_hbm(u) for u in us[:-3]] + us[-3:] for us in (x_units, y_units))
    x_plan, y_plan = (side, tuple(x_steps)), (side, tuple(y_steps))

    gathered = pltpu.VMEM((blocks, tok, width), BF16)
    loaded = pltpu.SemaphoreType.DMA((side,))
    values = pltpu.HBM((rows, tok, width), BF16)
    kept = pltpu.VMEM((tok, rows * width), F32)
    last = pltpu.VMEM((side + 1, width, rows * width), BF16)
    sums = pltpu.VMEM((blocks, tok, width), F32)
    hidden_most, grad_most, wi, li, lo, zeros = pl.pallas_call(
        functools.partial(early_kernel, ((side, x_plan[1][:-1]), (side, y_plan[1][:-1]))),
        out_shape=(kept, kept, pltpu.VMEM(w_in.shape, BF16), last, last, sums),
        out_specs=(vmem,) * 6,
        in_specs=[smem] + [anywhere] * (len(x_units) + len(y_units)),
        scratch_shapes=[
            pltpu.VMEM(w_out.shape, BF16),
            gathered,
            gathered,
            loaded,
            loaded,
            pltpu.SemaphoreType.DMA((2,)),
        ],
        compiler_params=params,
        name="early",
    )(where, *x_units[:-1], *y_units[:-1], in_hbm(w_in), in_hbm(w_out))
    placed, act, grad, _ = pl.pallas_call(
        back_kernel,
        out_shape=(pltpu.HBM((side, blocks // side, tok, width), BF16), values, values, sums),
        in_specs=[smem] + [vmem] * 8,
        out_specs=(anywhere, anywhere, anywhere, vmem),
        input_output_aliases={8: 3},
        scratch_shapes=[
            pltpu.VMEM((blocks, tok, width), BF16),
            pltpu.VMEM((rows, tok, width), BF16),
            pltpu.VMEM((rows, tok, width), BF16),
            pltpu.SemaphoreType.DMA((SLABS + 2,)),
        ],
        compiler_params=params,
        name="back",
    )(where, x_units[-1], y_units[-1], hidden_most, grad_most, wi, li, lo, zeros)

    on_ring = swap(placed, rings)

    half = jax.ShapeDtypeStruct((nx, 2, rows, each, width, width), BF16)
    own, other = pl.pallas_call(
        functools.partial(weight_kernel, (x_plan, y_plan)),
        out_shape=(half, half),
        in_specs=[smem] + [anywhere] * (len(x_units) + len(y_units) + 2),
        out_specs=(vmem, vmem),
        scratch_shapes=[
            gathered,
            gathered,
            pltpu.VMEM((rows, tok, width), BF16),
            pltpu.VMEM((rows, tok, width), BF16),
            loaded,
            loaded,
            pltpu.SemaphoreType.DMA((2,)),
        ],
        compiler_params=params,
        name="weights",
    )(where, *(in_hbm(v) for v in (*x_units, *y_units)), act, grad)
    swapped = lax.ppermute(other, "c", [(0, 1), (1, 0)])
    paired = [(own[d].astype(F32) + swapped[d].astype(F32)).astype(BF16) for d in range(nx)]
    spread = [
        lax.ppermute(paired[d], "x", [(i, (i + d) % nx) for i in range(nx)]) for d in range(1, nx)
    ]
    summed = sum((v.astype(F32) for v in spread), paired[0].astype(F32)).astype(BF16)

    on_line = pl.pallas_call(
        sum_kernel,
        out_shape=jax.ShapeDtypeStruct(on_ring.shape[1:], BF16),
        in_specs=[vmem],
        out_specs=vmem,
        compiler_params=params,
        name="sums",
    )(pltpu.with_memory_space_constraint(on_ring, pltpu.VMEM))
    received = swap(on_line, lines)
    grad_inputs = jnp.sum(received.astype(F32), axis=0).astype(BF16)
    return grad_inputs, summed[0], summed[1]


def solution(mesh):
    n_dp, n_blk = mesh.devices.shape
    sizes = (n_dp // 2, 2, 8, n_blk // 8)
    fine = Mesh(mesh.devices.reshape(sizes), ("x", "c", "y", "z"))
    dp, blk = ("x", "c"), ("y", "z")
    return jax.shard_map(
        functools.partial(per_device, sizes),
        mesh=fine,
        in_specs=(
            P(dp, blk),
            P(dp, blk),
            P(blk, None, None, None),
            P(blk, None),
            P(blk, None, None, None),
            P(blk, None),
        ),
        out_specs=(P(dp, blk), P(blk, dp, None, None), P(blk, dp, None, None)),
        check_vma=False,
    )
```

```python
import functools

import jax
import jax.numpy as jnp
from jax import lax
from jax.experimental import pallas as pl
from jax.experimental.pallas import tpu as pltpu
from jax.sharding import Mesh, PartitionSpec as P

BF16 = jnp.bfloat16
F32 = jnp.float32
GELU_SCALE = 0.7978845608028654
GELU_CUBE = 0.044715
VMEM_LIMIT = 36 * 1024 * 1024
SLABS = 8
CYZ = ("c", "y", "z")


def dot_nn(a, b):
    return lax.dot_general(a, b, (((1,), (0,)), ((), ())), preferred_element_type=F32)


def dot_nt(a, b):
    return lax.dot_general(a, b, (((1,), (1,)), ((), ())), preferred_element_type=F32)


def dot_tn(a, b):
    return lax.dot_general(a, b, (((0,), (0,)), ((), ())), preferred_element_type=F32)


def start_loads(where, units, into, sem, side):
    places = into.shape[0] // side
    loads = []
    for n, (ref, steps) in enumerate(units):
        place = lax.rem(where[2, 1] + (steps + places), places)
        loads.append(pltpu.make_async_copy(ref, into.at[pl.ds(place * side, side)], sem.at[n]))
        loads[-1].start()
    return loads


def row_of(blocks, where, line, r, per_row):
    return jnp.concatenate([blocks[where[line, r * per_row + k]] for k in range(per_row)], axis=1)


def early_kernel(plans, where, *refs):
    (side, x_steps), (_, y_steps) = plans
    n_x, n_y = len(x_steps), len(y_steps)
    x_units = list(zip(refs[:n_x], x_steps))
    y_units = list(zip(refs[n_x : n_x + n_y], y_steps))
    w_in, w_out = refs[n_x + n_y : n_x + n_y + 2]
    hidden, grad_act, wi, in_last, out_last, total, wo, x, y, x_sem, y_sem, w_sem = refs[n_x + n_y + 2 :]
    rows, per_row, width, _ = w_in.shape
    load_in = pltpu.make_async_copy(w_in, wi, w_sem.at[0])
    load_out = pltpu.make_async_copy(w_out, wo, w_sem.at[1])
    load_in.start()
    load_out.start()
    x_loads = start_loads(where, x_units, x, x_sem, side)
    y_loads = start_loads(where, y_units, y, y_sem, side)
    total[...] = jnp.zeros_like(total)
    in_last[...] = jnp.zeros_like(in_last)
    out_last[...] = jnp.zeros_like(out_last)
    places = x.shape[0] // side
    opposite = pl.ds(lax.rem(where[2, 1] + places // 2, places) * side, side)
    x[opposite] = jnp.zeros((side, *x.shape[1:]), BF16)
    y[opposite] = jnp.zeros((side, *y.shape[1:]), BF16)
    load_in.wait()
    load_out.wait()
    for r in range(rows):
        at = slice(r * width, (r + 1) * width)
        for k in range(per_row):
            in_last[where[3, r * per_row + k], :, at] = wi[r, k]
            out_last[where[4, r * per_row + k], :, at] = wo[r, k].T
    for copy in x_loads:
        copy.wait()
    for r in range(rows):
        x_row = row_of(x, where, 0, r, per_row)
        at = slice(r * width, (r + 1) * width)
        hidden[:, at] = dot_nn(x_row, wi[r].reshape(per_row * width, width))
    for copy in y_loads:
        copy.wait()
    for r in range(rows):
        w_row = jnp.concatenate([wo[r, k] for k in range(per_row)], axis=1)
        at = slice(r * width, (r + 1) * width)
        grad_act[:, at] = dot_nt(row_of(y, where, 1, r, per_row), w_row)


def back_kernel(where, x_last, y_last, hidden_most, grad_most, wi, li, lo, zeros, *refs):
    placed, act_out, grad_out, total, rounded, act, grad, out_sem = refs
    rows, per_row, width, _ = wi.shape
    blocks, side = total.shape[0], x_last.shape[0]
    x_unit = jnp.concatenate([x_last[n] for n in range(side)], axis=1)
    y_unit = jnp.concatenate([y_last[n] for n in range(side)], axis=1)
    hidden = hidden_most[...] + dot_nn(x_unit, li[:side].reshape(side * width, rows * width))
    grad_act = grad_most[...] + dot_nn(y_unit, lo[:side].reshape(side * width, rows * width))
    square = hidden * hidden
    tanh = jnp.tanh(GELU_SCALE * hidden * (1.0 + GELU_CUBE * square))
    half = 0.5 * (1.0 + tanh)
    slope = half + 0.5 * hidden * (1.0 - tanh * tanh) * (
        GELU_SCALE * (1.0 + 3.0 * GELU_CUBE * square)
    )
    activated = (hidden * half).astype(BF16)
    grad_hidden = (grad_act * slope).astype(BF16)
    for r in range(rows):
        at = slice(r * width, (r + 1) * width)
        act[r] = activated[:, at]
        grad[r] = grad_hidden[:, at]
    stores = [
        pltpu.make_async_copy(act, act_out, out_sem.at[SLABS]),
        pltpu.make_async_copy(grad, grad_out, out_sem.at[SLABS + 1]),
    ]
    for copy in stores:
        copy.start()
    for r in range(rows):
        at = slice(r * width, (r + 1) * width)
        terms = dot_nt(grad_hidden[:, at], wi[r].reshape(per_row * width, width))
        for k in range(per_row):
            c = where[0, r * per_row + k]
            total[c] = total[c] + terms[:, k * width : (k + 1) * width]
    slab = blocks // SLABS
    for s in range(SLABS):
        at = pl.ds(s * slab, slab)
        rounded[at] = total[at].astype(BF16)
        stores.append(pltpu.make_async_copy(rounded.at[at], placed.at[s], out_sem.at[s]))
        stores[-1].start()
    for copy in stores:
        copy.wait()


def weight_kernel(plans, where, *refs):
    (side, x_steps), (_, y_steps) = plans
    n_x, n_y = len(x_steps), len(y_steps)
    act_in, grad_in, own, other, x, y, act, grad, x_sem, y_sem, sem = refs[n_x + n_y :]
    loads = [
        pltpu.make_async_copy(act_in, act, sem.at[0]),
        pltpu.make_async_copy(grad_in, grad, sem.at[1]),
    ]
    for copy in loads:
        copy.start()
    loads += start_loads(where, list(zip(refs[:n_x], x_steps)), x, x_sem, side)
    loads += start_loads(where, list(zip(refs[n_x : n_x + n_y], y_steps)), y, y_sem, side)
    for copy in loads:
        copy.wait()
    xs, _, rows, each, width, _ = own.shape
    per_row = xs * 2 * each
    core = where[2, 0]
    for r in range(rows):
        act_t = act[r].T
        grad_r = grad[r]
        for away in range(xs):
            x_at = lax.rem(where[2, 2] + away, xs)
            for half, out in ((core, own), (1 - core, other)):
                for j in range(each):
                    at = r * per_row + (x_at * 2 + half) * each + j
                    out[away, 0, r, j] = dot_tn(x[where[0, at]], grad_r).astype(BF16)
                    out[away, 1, r, j] = dot_nn(act_t, y[where[1, at]]).astype(BF16)


def sum_kernel(parts, out, sums, sem):
    copies = []
    for n in range(parts.shape[1]):
        kept = parts[0, n].astype(F32)
        for s in range(1, parts.shape[0]):
            kept = kept + parts[s, n].astype(F32)
        sums[n] = kept.astype(BF16)
        copies.append(pltpu.make_async_copy(sums.at[n], out.at[n], sem.at[n]))
        copies[-1].start()
    for copy in copies:
        copy.wait()


def lines_and_rings(ny, nz):
    along_z = [[y * nz + z for z in range(nz)] for y in range(ny)]
    along_y = [[y * nz + z for y in range(ny)] for z in range(nz)]
    second = [[[ny * nz + p for p in group] for group in groups] for groups in (along_z, along_y)]
    return along_z + second[1], along_y + second[0]


def per_device(sizes, inputs, upstream, w_in, cols_in, w_out, cols_out):
    nx, nc, ny, nz = sizes
    side = nz
    tok, width = inputs.shape
    rows, per_row = cols_in.shape
    each = per_row // (nx * nc)
    blocks = ny * nz
    lines, rings = lines_and_rings(ny, nz)
    smem = pl.BlockSpec(memory_space=pltpu.SMEM)
    vmem = pl.BlockSpec(memory_space=pltpu.VMEM)
    anywhere = pl.BlockSpec(memory_space=pl.ANY)
    params = pltpu.CompilerParams(vmem_limit_bytes=VMEM_LIMIT)

    def in_hbm(values):
        return pltpu.with_memory_space_constraint(values, pltpu.HBM)

    def swap(values, groups):
        return lax.all_to_all(
            values, CYZ, split_axis=0, concat_axis=0, tiled=True, axis_index_groups=groups
        )

    def turn(values, by):
        pairs = [(g[i], g[(i + by) % side]) for g in rings for i in range(side)]
        return lax.ppermute(values, CYZ, pairs)

    core, y_at, z_at = (lax.axis_index(a) for a in CYZ)
    cols = jnp.stack([cols_in.reshape(-1), cols_out.reshape(-1)])
    cols = jnp.where(core == 0, cols, cols % nz * ny + cols // nz)
    place = jnp.where(core == 0, y_at, z_at)
    here = jnp.stack([core, place, lax.axis_index("x")]).astype(jnp.int32)
    here = jnp.pad(here, (0, rows * per_row - 3)).reshape(1, -1)
    opposite = (place + ny // 2) % ny
    lasts = jnp.where(cols // side == opposite, cols % side, side)
    where = jnp.concatenate([cols, here, lasts])

    mine = jnp.stack([inputs, upstream])
    unit = swap(jnp.broadcast_to(mine, (side, *mine.shape)), lines)
    x_units, y_units = [unit[:, 0]], [unit[:, 1]]
    x_steps, y_steps = [0], [0]
    x_ahead = x_back = x_units[0]
    y_ahead = y_back = y_units[0]
    for s in range(1, side // 2):
        x_ahead, x_back = turn(x_ahead, 1), turn(x_back, -1)
        y_back, y_ahead = turn(y_back, -1), turn(y_ahead, 1)
        x_units += [x_ahead, x_back]
        y_units += [y_ahead, y_back]
        x_steps += [-s, s]
        y_steps += [-s, s]
    x_units.append(turn(x_ahead, 1))
    y_units.append(turn(y_back, -1))
    x_steps.append(-(side // 2))
    y_steps.append(side // 2)
    x_units, y_units = ([in_hbm(u) for u in us[:-3]] + us[-3:] for us in (x_units, y_units))
    x_plan, y_plan = (side, tuple(x_steps)), (side, tuple(y_steps))

    gathered = pltpu.VMEM((blocks, tok, width), BF16)
    loaded = pltpu.SemaphoreType.DMA((side,))
    values = pltpu.HBM((rows, tok, width), BF16)
    kept = pltpu.VMEM((tok, rows * width), F32)
    last = pltpu.VMEM((side + 1, width, rows * width), BF16)
    sums = pltpu.VMEM((blocks, tok, width), F32)
    hidden_most, grad_most, wi, li, lo, zeros = pl.pallas_call(
        functools.partial(early_kernel, ((side, x_plan[1][:-1]), (side, y_plan[1][:-1]))),
        out_shape=(kept, kept, pltpu.VMEM(w_in.shape, BF16), last, last, sums),
        out_specs=(vmem,) * 6,
        in_specs=[smem] + [anywhere] * (len(x_units) + len(y_units)),
        scratch_shapes=[
            pltpu.VMEM(w_out.shape, BF16),
            gathered,
            gathered,
            loaded,
            loaded,
            pltpu.SemaphoreType.DMA((2,)),
        ],
        compiler_params=params,
        name="early",
    )(where, *x_units[:-1], *y_units[:-1], in_hbm(w_in), in_hbm(w_out))
    placed, act, grad, _ = pl.pallas_call(
        back_kernel,
        out_shape=(pltpu.HBM((side, blocks // side, tok, width), BF16), values, values, sums),
        in_specs=[smem] + [vmem] * 8,
        out_specs=(anywhere, anywhere, anywhere, vmem),
        input_output_aliases={8: 3},
        scratch_shapes=[
            pltpu.VMEM((blocks, tok, width), BF16),
            pltpu.VMEM((rows, tok, width), BF16),
            pltpu.VMEM((rows, tok, width), BF16),
            pltpu.SemaphoreType.DMA((SLABS + 2,)),
        ],
        compiler_params=params,
        name="back",
    )(where, x_units[-1], y_units[-1], hidden_most, grad_most, wi, li, lo, zeros)

    on_ring = swap(placed, rings)

    half = jax.ShapeDtypeStruct((nx, 2, rows, each, width, width), BF16)
    own, other = pl.pallas_call(
        functools.partial(weight_kernel, (x_plan, y_plan)),
        out_shape=(half, half),
        in_specs=[smem] + [anywhere] * (len(x_units) + len(y_units) + 2),
        out_specs=(vmem, vmem),
        scratch_shapes=[
            gathered,
            gathered,
            pltpu.VMEM((rows, tok, width), BF16),
            pltpu.VMEM((rows, tok, width), BF16),
            loaded,
            loaded,
            pltpu.SemaphoreType.DMA((2,)),
        ],
        compiler_params=params,
        name="weights",
    )(where, *(in_hbm(v) for v in (*x_units, *y_units)), act, grad)
    swapped = lax.ppermute(other, "c", [(0, 1), (1, 0)])
    paired = [(own[d].astype(F32) + swapped[d].astype(F32)).astype(BF16) for d in range(nx)]
    spread = [
        lax.ppermute(paired[d], "x", [(i, (i + d) % nx) for i in range(nx)]) for d in range(1, nx)
    ]
    summed = sum((v.astype(F32) for v in spread), paired[0].astype(F32)).astype(BF16)

    on_line = pl.pallas_call(
        sum_kernel,
        out_shape=pltpu.HBM((blocks // side, tok, width), BF16),
        in_specs=[vmem],
        out_specs=anywhere,
        scratch_shapes=[pltpu.VMEM((blocks // side, tok, width), BF16), loaded],
        compiler_params=params,
        name="sums",
    )(pltpu.with_memory_space_constraint(on_ring, pltpu.VMEM))
    received = swap(on_line, lines)
    grad_inputs = jnp.sum(received.astype(F32), axis=0).astype(BF16)
    return grad_inputs, summed[0], summed[1]


def solution(mesh):
    n_dp, n_blk = mesh.devices.shape
    sizes = (n_dp // 2, 2, 8, n_blk // 8)
    fine = Mesh(mesh.devices.reshape(sizes), ("x", "c", "y", "z"))
    dp, blk = ("x", "c"), ("y", "z")
    return jax.shard_map(
        functools.partial(per_device, sizes),
        mesh=fine,
        in_specs=(
            P(dp, blk),
            P(dp, blk),
            P(blk, None, None, None),
            P(blk, None),
            P(blk, None, None, None),
            P(blk, None),
        ),
        out_specs=(P(dp, blk), P(blk, dp, None, None), P(blk, dp, None, None)),
        check_vma=False,
    )
```
